32 devices in a mesh: seg: 8 (over z, y), rep: 4 (over x, core).
Axes of the slice: x: 2, y: 2, z: 4, core: 2. Of those that a mesh axis runs over, the one named last changes fastest.
Arguments:
- tokens: bfloat16 [4, 2048, 1024], P('rep', 'seg'), may hold values from -6 to 6
- cotangent: bfloat16 [4, 2048, 1024], P('rep', 'seg'), may hold values from -6 to 6
- coefficients: bfloat16 [4, 8, 32], P('rep'), may hold values from 0 to 1, as said below
- w_gate: bfloat16 [32, 1024, 512], P(None, 'seg'), may hold values from -0.1875 to 0.1875
- w_up: bfloat16 [32, 1024, 512], P(None, 'seg'), may hold values from -0.1875 to 0.1875
- w_down: bfloat16 [32, 1024, 512], P(None, 'seg'), may hold values from -0.25 to 0.25
Outputs:
- input_grad: bfloat16 [4, 2048, 1024], P('rep', 'seg')
- grad_gate: bfloat16 [32, 1024, 512], P('rep', 'seg')
- grad_up: bfloat16 [32, 1024, 512], P('rep', 'seg')
- grad_down: bfloat16 [32, 1024, 512], P('rep', 'seg')
The draws below stay inside these ranges and needn't reach their ends.
Inputs may be any that keep to these rules, and one draw needn't show every extreme that they name: Each segment's coefficients are positive and sum to 1 over the 32 experts, up to bfloat16 rounding.
All inputs are finite; a program needn't handle non-finite values.
Results may differ from the reference program's by a relative error of at most 0.0072.
Values may be sent and summed in bfloat16 or wider, within the bound.
A program may use at most 128 MiB of HBM per device.

```python
import jax
import jax.numpy as jnp
from jax import lax

D = 1024
H = 512
E = 32
SEG_LEN = 256
REPS = 4
SEGS = 8
TOK_REP = 2048


def draw_coefficients(key, part):
    first_key, second_key = jax.random.split(jax.random.fold_in(key, 7))
    replica_bias = 0.5 * jax.random.normal(second_key, (REPS, 1, E), jnp.float32)
    logits = 2.0 * jax.random.normal(first_key, (REPS, SEGS, E), jnp.float32)
    return jax.nn.softmax(logits + replica_bias, axis=-1).astype(jnp.bfloat16)


def block_levels(own_key, shape, cuts, least, high):
    gain = 1.0
    for position, parts in cuts:
        draws = jax.random.uniform(jax.random.fold_in(jax.random.fold_in(own_key, 6), position), (parts,), jnp.float32, least / len(cuts), high / len(cuts))
        gain = gain * jnp.repeat(jnp.exp(draws), shape[position] // parts).reshape((-1,) + (1,) * (len(shape) - 1 - position))
    return gain


def noise(rng, dims, width, most, cuts=(), held_as=jnp.bfloat16):
    entries = width * jax.random.normal(rng, dims, jnp.float32)
    if cuts:
        entries = entries * block_levels(rng, dims, cuts, -0.22, 0.18)
    return jnp.clip(entries, -most, most).astype(held_as)


def setup_inputs(seed: int = 0) -> dict:
    key_list = jax.random.split(jax.random.key(seed), 7)
    tokens = noise(key_list[0], (REPS, TOK_REP, D), 1.0, 6.0, ((0, 4), (1, 8)))
    cotangent = noise(key_list[1], (REPS, TOK_REP, D), 1.0, 6.0, ((0, 4), (1, 8)))
    coefficients = draw_coefficients(jax.random.fold_in(key_list[6], 71), 0)
    w_gate = noise(key_list[3], (E, D, H), D ** -0.5, 0.1875, ((1, 8),))
    w_up = noise(key_list[4], (E, D, H), D ** -0.5, 0.1875, ((1, 8),))
    w_down = noise(key_list[5], (E, D, H), H ** -0.5, 0.25, ((1, 8),))
    return dict(tokens=tokens, cotangent=cotangent, coefficients=coefficients, w_gate=w_gate, w_up=w_up, w_down=w_down)


def segment_pass(carry, inputs):
    segment_x, segment_g, weights_row = inputs
    stacked = carry[1]
    weights_wide = weights_row.astype(jnp.float32)
    merged = jnp.einsum("e,kem->km", weights_wide, stacked.astype(jnp.float32), precision=lax.Precision.HIGHEST)
    merged = merged.astype(jnp.bfloat16).reshape(3, D, H)
    merged_gate = merged[0]
    merged_up = merged[1]
    merged_down = merged[2]
    gate_proj = jnp.dot(segment_x, merged_gate, preferred_element_type=jnp.float32)
    up_proj = jnp.dot(segment_x, merged_up, preferred_element_type=jnp.float32)
    sigma = jax.nn.sigmoid(gate_proj)
    activated = gate_proj * sigma
    hidden = (activated * up_proj).astype(jnp.bfloat16)
    d_hidden = jnp.dot(segment_g, merged_down, preferred_element_type=jnp.float32)
    d_gate = (d_hidden * up_proj * sigma * (1.0 + gate_proj * (1.0 - sigma))).astype(jnp.bfloat16)
    d_up = (d_hidden * activated).astype(jnp.bfloat16)
    input_grad = jnp.dot(d_gate, merged_gate.T, preferred_element_type=jnp.float32)
    input_grad = (input_grad + jnp.dot(d_up, merged_up.T, preferred_element_type=jnp.float32)).astype(jnp.bfloat16)
    m_gate = jnp.dot(segment_x.T, d_gate, preferred_element_type=jnp.float32).astype(jnp.bfloat16)
    m_up = jnp.dot(segment_x.T, d_up, preferred_element_type=jnp.float32).astype(jnp.bfloat16)
    m_down = jnp.dot(segment_g.T, hidden, preferred_element_type=jnp.float32).astype(jnp.bfloat16)
    grads = jnp.stack([m_gate, m_up, m_down]).reshape(3, 1, D * H).astype(jnp.float32)
    accumulated = carry[0] + weights_wide[None, :, None] * grads
    return (accumulated, stacked), input_grad


def reference(tokens, cotangent, coefficients, w_gate, w_up, w_down):
    stacked = jnp.stack([w_gate, w_up, w_down]).reshape(3, E, D * H)
    segment_xs = tokens.reshape(REPS * SEGS, SEG_LEN, D)
    segment_gs = cotangent.reshape(REPS * SEGS, SEG_LEN, D)
    rows = coefficients.reshape(REPS * SEGS, E)
    start = jnp.zeros((3, E, D * H), jnp.float32)
    (accumulated, unused), input_grads = lax.scan(segment_pass, (start, stacked), (segment_xs, segment_gs, rows))
    input_grad = input_grads.reshape(REPS, TOK_REP, D)
    grads = accumulated.astype(jnp.bfloat16).reshape(3, E, D, H)
    return input_grad, grads[0], grads[1], grads[2]
```

```python
import functools

import jax
import jax.numpy as jnp
from jax import lax
from jax.experimental import pallas as pl
from jax.experimental.pallas import tpu as pltpu
from jax.sharding import PartitionSpec as P

MESH = pl.DeviceIdType.MESH
F32 = jnp.float32
BF16 = jnp.bfloat16
T = 16
GATE, UP, DOWN = 0, 1, 2


def one_hot(shape, rows_of, columns_of):
    row = lax.broadcasted_iota(jnp.int32, shape, 0)
    column = lax.broadcasted_iota(jnp.int32, shape, 1)
    return rows_of(row) == columns_of(column)


def dot(a, b):
    return jnp.dot(a, b, preferred_element_type=F32)


def dot_t(a, b):
    return lax.dot_general(a, b, (((1,), (1,)), ((), ())), preferred_element_type=F32)


def kernel(
    S, R, coef_ref, tok_hbm, cot_hbm, wg_hbm, wu_hbm, wd_hbm,
    ig_hbm, gg_hbm, gu_hbm, gd_hbm,
    x, g, xt, gt, w, msend, mfull, gsend, gall, outv, igv, cbuf, mix, fold,
    gate_s, up_s, dh_s, hid_s, dgate_s, dup_s,
    load_sem, out_sem, fsend, frecv, bsend, brecv, xsend, xrecv, ssend, srecv, csend, crecv,
):
    me = lax.axis_index("seg")
    rep = lax.axis_index("rep")
    E, rows, H = w.shape[1:]
    EL = outv.shape[1]
    chips = R // 2
    sibling = rep + 1 - 2 * lax.rem(rep, 2)

    def seg_at(k):
        return lax.rem(me + k, S)

    def seg_from(k):
        return lax.rem(me - k + S, S)

    def rep_at(k):
        return lax.rem(rep + k, R)

    def rep_from(k):
        return lax.rem(rep - k + R, R)

    def loop(lo, hi, body):
        lax.fori_loop(lo, hi, lambda i, c: (body(i), c)[1], 0)

    loads = [pltpu.make_async_copy(tok_hbm.at[0], x, load_sem.at[0]),
             pltpu.make_async_copy(cot_hbm.at[0], g, load_sem.at[1])]
    w_loads = [pltpu.make_async_copy(h, w.at[p], load_sem.at[2 + p])
               for p, h in enumerate((wg_hbm, wu_hbm, wd_hbm))]
    for c in w_loads + loads:
        c.start()

    barrier = pltpu.get_barrier_semaphore()
    for k in range(1, S):
        pl.semaphore_signal(barrier, inc=1, device_id={"seg": seg_at(k)}, device_id_type=MESH)
    for k in range(1, R):
        pl.semaphore_signal(barrier, inc=1, device_id={"rep": rep_at(k)}, device_id_type=MESH)

    coef = coef_ref[0].astype(F32)
    LANES = cbuf.shape[2]
    cbuf[rep] = dot(coef, one_hot((E, LANES), lambda i: i, lambda j: j).astype(F32))
    tall = dot(one_hot((S * T, S), lambda i: i // T, lambda j: j).astype(F32), coef)
    wide = dot(tall, one_hot((E, E * T), lambda i: i, lambda j: j // T).astype(F32))
    keep = one_hot((S * T, E * T), lambda i: i % T, lambda j: j % T)
    mix[...] = jnp.where(keep, wide, 0.0).astype(BF16)

    pl.semaphore_wait(barrier, S - 1 + R - 1)

    def coef_copy(k, owner):
        return pltpu.make_async_remote_copy(
            src_ref=cbuf.at[owner], dst_ref=cbuf.at[owner],
            send_sem=csend.at[k], recv_sem=crecv.at[k],
            device_id={"rep": rep_at(k)}, device_id_type=MESH)

    for k in range(1, R):
        coef_copy(k, rep).start()

    def merged_copy(p, k, owner):
        at = pl.ds(pl.multiple_of(owner * rows, rows), rows)
        return pltpu.make_async_remote_copy(
            src_ref=msend.at[p, seg_at(k)], dst_ref=mfull.at[p, at],
            send_sem=fsend.at[p, k], recv_sem=frecv.at[p, k],
            device_id={"seg": seg_at(k)}, device_id_type=MESH)

    for p in (GATE, UP, DOWN):
        w_loads[p].wait()

        def merge(b, p=p):
            at = pl.ds(pl.multiple_of(b * T, T), T)
            block = dot(mix[...], w[p, :, at, :].reshape(E * T, H))
            msend[p, :, at, :] = block.astype(BF16).reshape(S, T, H)

        loop(0, rows // T, merge)
        loop(1, S, lambda k, p=p: merged_copy(p, k, me).start())
        mfull[p, pl.ds(pl.multiple_of(me * rows, rows), rows), :] = msend[p, me]

    for c in loads:
        c.wait()
    xt[...] = x[...].T
    gt[...] = g[...].T
    for k in range(1, R):
        coef_copy(k, rep_from(k)).wait_recv()
    every = cbuf[...].reshape(R * S, LANES)
    mine = one_hot((EL * T, LANES), lambda i: i // T + rep * EL, lambda j: j).astype(F32)
    tall = dot_t(mine, every)
    wide = dot(tall, one_hot((R * S, R * S * T), lambda i: i, lambda j: j // T).astype(F32))
    keep = one_hot((EL * T, R * S * T), lambda i: i % T, lambda j: j % T)
    fold[...] = jnp.where(keep, wide, 0.0).astype(BF16)

    def grad_copy(p, k, owner):
        return pltpu.make_async_remote_copy(
            src_ref=gsend.at[p, k], dst_ref=gall.at[p, rep, owner],
            send_sem=bsend.at[p, k], recv_sem=brecv.at[p, k],
            device_id={"seg": seg_at(k)}, device_id_type=MESH)

    def chip_copy(p, j, k, owner):
        block = gall.at[p, owner, seg_from(k)]
        return pltpu.make_async_remote_copy(
            src_ref=block, dst_ref=block,
            send_sem=xsend.at[p, j, k], recv_sem=xrecv.at[p, j, k],
            device_id={"rep": rep_at(2 * j)}, device_id_type=MESH)

    def sibling_copy(p, j, k, owner):
        block = gall.at[p, owner, seg_from(k)]
        return pltpu.make_async_remote_copy(
            src_ref=block, dst_ref=block,
            send_sem=ssend.at[p, j, k], recv_sem=srecv.at[p, j, k],
            device_id={"rep": sibling}, device_id_type=MESH)

    def pass_on(p, k):
        for j in range(1, chips):
            chip_copy(p, j, k, rep).start()
        sibling_copy(p, 0, k, rep).start()

    def send_grads(p, transposed, right):
        def one(k):
            at = pl.ds(pl.multiple_of(seg_at(k) * rows, rows), rows)
            return dot(transposed[at, :], right[...]).astype(BF16)

        def step(k):
            gsend[p, k] = one(k)
            grad_copy(p, k, me).start()

        loop(1, S, step)
        gall[p, rep, me] = one(0)
        pass_on(p, 0)

    loop(1, S, lambda k: merged_copy(GATE, k, seg_from(k)).wait_recv())
    gate_s[...] = dot(x[...], mfull[GATE])
    loop(1, S, lambda k: merged_copy(UP, k, seg_from(k)).wait_recv())
    up_s[...] = dot(x[...], mfull[UP])
    CH = 32
    tokens = x.shape[0]

    def hidden(i):
        at = pl.ds(pl.multiple_of(i * CH, CH), CH)
        gate = gate_s[at, :]
        hid_s[at, :] = (gate * jax.nn.sigmoid(gate) * up_s[at, :]).astype(BF16)

    loop(0, tokens // CH, hidden)
    send_grads(DOWN, gt, hid_s)

    loop(1, S, lambda k: merged_copy(DOWN, k, seg_from(k)).wait_recv())
    dh_s[...] = dot(g[...], mfull[DOWN])

    def backward(i):
        at = pl.ds(pl.multiple_of(i * CH, CH), CH)
        gate = gate_s[at, :]
        dh = dh_s[at, :]
        sigma = jax.nn.sigmoid(gate)
        dgate_s[at, :] = (dh * up_s[at, :] * sigma * (1.0 + gate * (1.0 - sigma))).astype(BF16)
        dup_s[at, :] = (dh * (gate * sigma)).astype(BF16)

    loop(0, tokens // CH, backward)
    send_grads(GATE, xt, dgate_s)
    send_grads(UP, xt, dup_s)

    def input_grad(i):
        at = pl.ds(pl.multiple_of(i * rows, rows), rows)
        total = dot_t(dgate_s[...], mfull[GATE, at, :]) + dot_t(dup_s[...], mfull[UP, at, :])
        igv[:, at] = total.astype(BF16)

    loop(0, S, input_grad)
    ig_copy = pltpu.make_async_copy(igv, ig_hbm.at[0], out_sem.at[3])
    ig_copy.start()

    outs = (gg_hbm, gu_hbm, gd_hbm)
    out_copies = []
    for p in (DOWN, GATE, UP):
        def arrived(k, p=p):
            grad_copy(p, k, seg_from(k)).wait_recv()
            pass_on(p, k)

        loop(1, S, arrived)

        def from_chip(k, p=p):
            for j in range(1, chips):
                owner = rep_from(2 * j)
                chip_copy(p, j, k, owner).wait_recv()
                sibling_copy(p, j, k, owner).start()

        loop(0, S, from_chip)

        def from_sibling(k, p=p):
            for j in range(chips):
                sibling_copy(p, j, k, lax.rem(sibling - 2 * j + R, R)).wait_recv()

        loop(0, S, from_sibling)

        def folded(b, p=p):
            at = pl.ds(pl.multiple_of(b * T, T), T)
            block = dot(fold[...], gall[p, :, :, at, :].reshape(R * S * T, H))
            outv[p, :, at, :] = block.astype(BF16).reshape(EL, T, H)

        loop(0, rows // T, folded)
        c = pltpu.make_async_copy(outv.at[p], outs[p], out_sem.at[p])
        c.start()
        out_copies.append(c)

    for k in range(1, R):
        coef_copy(k, rep).wait_send()
    for p in (GATE, UP, DOWN):
        def sent(k, p=p):
            merged_copy(p, k, me).wait_send()
            grad_copy(p, k, me).wait_send()

        loop(1, S, sent)

        def passed(k, p=p):
            for j in range(1, chips):
                chip_copy(p, j, k, rep).wait_send()
            for j in range(chips):
                sibling_copy(p, j, k, rep_from(2 * j)).wait_send()

        loop(0, S, passed)
    ig_copy.wait()
    for c in out_copies:
        c.wait()


def fused(S, R, tokens, cotangent, coefficients, w_gate, w_up, w_down):
    E, rows, H = w_gate.shape
    L, D = tokens.shape[1:]
    EL = E // R
    chips = R // 2
    lanes = -(-E // 128) * 128
    any_spec = pl.BlockSpec(memory_space=pl.ANY)
    dma = pltpu.SemaphoreType.DMA
    vmem = pltpu.VMEM
    grad = jax.ShapeDtypeStruct((EL, rows, H), BF16)
    flops = 16 * L * D * H + 2 * 3 * T * rows * H * E * S + 2 * 3 * T * rows * H * EL * R * S
    return pl.pallas_call(
        functools.partial(kernel, S, R),
        out_shape=(jax.ShapeDtypeStruct((1, L, D), BF16), grad, grad, grad),
        in_specs=[pl.BlockSpec(memory_space=vmem)] + [any_spec] * 5,
        out_specs=(any_spec,) * 4,
        scratch_shapes=[
            vmem((L, D), BF16), vmem((L, D), BF16), vmem((D, L), BF16), vmem((D, L), BF16),
            vmem((3, E, rows, H), BF16),
            vmem((3, S, rows, H), BF16),
            vmem((3, D, H), BF16),
            vmem((3, S, rows, H), BF16),
            vmem((3, R, S, rows, H), BF16),
            vmem((3, EL, rows, H), BF16),
            vmem((L, D), BF16),
            vmem((R, S, lanes), F32),
            vmem((S * T, E * T), BF16),
            vmem((EL * T, R * S * T), BF16),
            vmem((L, H), F32), vmem((L, H), F32), vmem((L, H), F32),
            vmem((L, H), BF16), vmem((L, H), BF16), vmem((L, H), BF16),
            dma((5,)), dma((4,)),
            dma((3, S)), dma((3, S)), dma((3, S)), dma((3, S)),
            dma((3, chips, S)), dma((3, chips, S)), dma((3, chips, S)), dma((3, chips, S)),
            dma((R,)), dma((R,)),
        ],
        compiler_params=pltpu.CompilerParams(
            collective_id=0, has_side_effects=True, vmem_limit_bytes=58 * 1024 * 1024),
        cost_estimate=pl.CostEstimate(
            flops=flops, bytes_accessed=2 * (3 * E * rows * H + 3 * L * D + 3 * EL * rows * H),
            transcendentals=2 * L * H),
    )(coefficients, tokens, cotangent, w_gate, w_up, w_down)


def local(tokens, cotangent, coefficients, w_gate, w_up, w_down):
    mixing = coefficients[0]
    stacked = jnp.stack([w_gate, w_up, w_down])
    merged = jnp.einsum(
        "se,kedh->ksdh", mixing, stacked, preferred_element_type=jnp.float32
    ).astype(jnp.bfloat16)
    arrived = lax.all_to_all(merged, "seg", split_axis=1, concat_axis=2, tiled=True)
    merged_gate = arrived[0, 0]
    merged_up = arrived[1, 0]
    merged_down = arrived[2, 0]
    segment_x = tokens[0]
    segment_g = cotangent[0]
    contract = (((0,), (0,)), ((), ()))
    transposed = (((1,), (1,)), ((), ()))

    def fold_experts(pieces):
        return jnp.einsum("se,ksdh->kedh", mixing, pieces, preferred_element_type=jnp.float32)

    gate_proj = jnp.dot(segment_x, merged_gate, preferred_element_type=jnp.float32)
    up_proj = jnp.dot(segment_x, merged_up, preferred_element_type=jnp.float32)
    sigma = jax.nn.sigmoid(gate_proj)
    activated = gate_proj * sigma
    hidden = (activated * up_proj).astype(jnp.bfloat16)
    grad_down_seg = lax.dot_general(
        segment_g, hidden, contract, preferred_element_type=jnp.float32
    ).astype(jnp.bfloat16)
    down_folded = fold_experts(
        lax.all_to_all(grad_down_seg[None, None], "seg", split_axis=2, concat_axis=1, tiled=True)
    )
    down_summed = lax.psum_scatter(down_folded, "rep", scatter_dimension=1, tiled=True)
    d_hidden = jnp.dot(segment_g, merged_down, preferred_element_type=jnp.float32)
    d_gate = (d_hidden * up_proj * sigma * (1.0 + gate_proj * (1.0 - sigma))).astype(jnp.bfloat16)
    d_up = (d_hidden * activated).astype(jnp.bfloat16)
    input_grad = lax.dot_general(
        d_gate, merged_gate, transposed, preferred_element_type=jnp.float32
    )
    input_grad = input_grad + lax.dot_general(
        d_up, merged_up, transposed, preferred_element_type=jnp.float32
    )
    input_grad = input_grad.astype(jnp.bfloat16)
    grad_gate_seg = lax.dot_general(
        segment_x, d_gate, contract, preferred_element_type=jnp.float32
    ).astype(jnp.bfloat16)
    grad_up_seg = lax.dot_general(
        segment_x, d_up, contract, preferred_element_type=jnp.float32
    ).astype(jnp.bfloat16)
    pair = jnp.stack([grad_gate_seg, grad_up_seg])[:, None]
    pair_folded = fold_experts(lax.all_to_all(pair, "seg", split_axis=2, concat_axis=1, tiled=True))
    pair_summed = lax.psum_scatter(pair_folded, "rep", scatter_dimension=1, tiled=True)
    summed = jnp.concatenate([pair_summed, down_summed], axis=0)
    grads = summed.astype(jnp.bfloat16)
    return (input_grad[None], grads[0], grads[1], grads[2])


def solution(mesh):
    placed = (
        P("rep", "seg", None),
        P("rep", "seg", None),
        P("rep", None, None),
        P(None, "seg", None),
        P(None, "seg", None),
        P(None, "seg", None),
    )
    S, R = mesh.shape["seg"], mesh.shape["rep"]

    def body(tokens, cotangent, coefficients, w_gate, w_up, w_down):
        args = (tokens, cotangent, coefficients, w_gate, w_up, w_down)
        if w_gate.shape[1] % 128 == 0 and R % 2 == 0 and tokens.shape[1] % 128 == 0:
            return fused(S, R, *args)
        return local(*args)

    return jax.shard_map(
        body,
        mesh=mesh,
        in_specs=placed,
        out_specs=(
            P("rep", "seg", None),
            P("rep", "seg", None),
            P("rep", "seg", None),
            P("rep", "seg", None),
        ),
        check_vma=False,
    )
```

```python
import functools

import jax
import jax.numpy as jnp
from jax import lax
from jax.experimental import pallas as pl
from jax.experimental.pallas import tpu as pltpu
from jax.sharding import PartitionSpec as P

MESH = pl.DeviceIdType.MESH
F32 = jnp.float32
BF16 = jnp.bfloat16
T = 16
GATE, UP, DOWN = 0, 1, 2


def one_hot(shape, rows_of, columns_of):
    row = lax.broadcasted_iota(jnp.int32, shape, 0)
    column = lax.broadcasted_iota(jnp.int32, shape, 1)
    return rows_of(row) == columns_of(column)


def dot(a, b):
    return jnp.dot(a, b, preferred_element_type=F32)


def dot_t(a, b):
    return lax.dot_general(a, b, (((1,), (1,)), ((), ())), preferred_element_type=F32)


def kernel(
    S, R, coef_ref, tok_hbm, cot_hbm, wg_hbm, wu_hbm, wd_hbm,
    ig_hbm, gg_hbm, gu_hbm, gd_hbm,
    x, g, xt, gt, w, msend, mfull, gsend, gall, outv, igv, cbuf, mix, fold,
    gate_s, up_s, dh_s, hid_s, dgate_s, dup_s,
    load_sem, out_sem, fsend, frecv, bsend, brecv, xsend, xrecv, ssend, srecv, csend, crecv,
):
    me = lax.axis_index("seg")
    rep = lax.axis_index("rep")
    E, rows, H = w.shape[1:]
    EL = outv.shape[1]
    chips = R // 2
    sibling = rep + 1 - 2 * lax.rem(rep, 2)

    def seg_at(k):
        return lax.rem(me + k, S)

    def seg_from(k):
        return lax.rem(me - k + S, S)

    def rep_at(k):
        return lax.rem(rep + k, R)

    def rep_from(k):
        return lax.rem(rep - k + R, R)

    def loop(lo, hi, body):
        lax.fori_loop(lo, hi, lambda i, c: (body(i), c)[1], 0)

    loads = [pltpu.make_async_copy(tok_hbm.at[0], x, load_sem.at[0]),
             pltpu.make_async_copy(cot_hbm.at[0], g, load_sem.at[1])]
    w_loads = [pltpu.make_async_copy(h, w.at[p], load_sem.at[2 + p])
               for p, h in enumerate((wg_hbm, wu_hbm, wd_hbm))]
    for c in w_loads + loads:
        c.start()

    barrier = pltpu.get_barrier_semaphore()
    for k in range(1, S):
        pl.semaphore_signal(barrier, inc=1, device_id={"seg": seg_at(k)}, device_id_type=MESH)
    for k in range(1, R):
        pl.semaphore_signal(barrier, inc=1, device_id={"rep": rep_at(k)}, device_id_type=MESH)

    coef = coef_ref[0].astype(F32)
    LANES = cbuf.shape[2]
    cbuf[rep] = dot(coef, one_hot((E, LANES), lambda i: i, lambda j: j).astype(F32))
    tall = dot(one_hot((S * T, S), lambda i: i // T, lambda j: j).astype(F32), coef)
    wide = dot(tall, one_hot((E, E * T), lambda i: i, lambda j: j // T).astype(F32))
    keep = one_hot((S * T, E * T), lambda i: i % T, lambda j: j % T)
    mix[...] = jnp.where(keep, wide, 0.0).astype(BF16)

    pl.semaphore_wait(barrier, S - 1 + R - 1)

    def coef_copy(k, owner):
        return pltpu.make_async_remote_copy(
            src_ref=cbuf.at[owner], dst_ref=cbuf.at[owner],
            send_sem=csend.at[k], recv_sem=crecv.at[k],
            device_id={"rep": rep_at(k)}, device_id_type=MESH)

    for k in range(1, R):
        coef_copy(k, rep).start()

    def merged_copy(p, k, owner):
        at = pl.ds(pl.multiple_of(owner * rows, rows), rows)
        return pltpu.make_async_remote_copy(
            src_ref=msend.at[p, seg_at(k)], dst_ref=mfull.at[p, at],
            send_sem=fsend.at[p, k], recv_sem=frecv.at[p, k],
            device_id={"seg": seg_at(k)}, device_id_type=MESH)

    for p in (GATE, UP, DOWN):
        w_loads[p].wait()

        def merge(b, p=p):
            at = pl.ds(pl.multiple_of(b * T, T), T)
            block = dot(mix[...], w[p, :, at, :].reshape(E * T, H))
            msend[p, :, at, :] = block.astype(BF16).reshape(S, T, H)

        loop(0, rows // T, merge)
        if p == GATE:
            loop(1, S, lambda k: merged_copy(GATE, k, me).start())
        mfull[p, pl.ds(pl.multiple_of(me * rows, rows), rows), :] = msend[p, me]

    for c in loads:
        c.wait()
    xt[...] = x[...].T
    gt[...] = g[...].T
    for k in range(1, R):
        coef_copy(k, rep_from(k)).wait_recv()
    every = cbuf[...].reshape(R * S, LANES)
    mine = one_hot((EL * T, LANES), lambda i: i // T + rep * EL, lambda j: j).astype(F32)
    tall = dot_t(mine, every)
    wide = dot(tall, one_hot((R * S, R * S * T), lambda i: i, lambda j: j // T).astype(F32))
    keep = one_hot((EL * T, R * S * T), lambda i: i % T, lambda j: j % T)
    fold[...] = jnp.where(keep, wide, 0.0).astype(BF16)

    def send_after(p, before):
        def step(k):
            merged_copy(before, k, me).wait_send()
            merged_copy(p, k, me).start()

        loop(1, S, step)

    Q = bsend.shape[1]
    part = rows // Q

    def piece(c):
        return pl.ds(c * part, part)

    def grad_copy(p, c, k, owner):
        return pltpu.make_async_remote_copy(
            src_ref=gsend.at[p, k, piece(c)], dst_ref=gall.at[p, rep, owner, piece(c)],
            send_sem=bsend.at[p, c, k], recv_sem=brecv.at[p, c, k],
            device_id={"seg": seg_at(k)}, device_id_type=MESH)

    def chip_copy(p, c, j, owner):
        block = gall.at[p, owner, :, piece(c)]
        return pltpu.make_async_remote_copy(
            src_ref=block, dst_ref=block,
            send_sem=xsend.at[p, c, j], recv_sem=xrecv.at[p, c, j],
            device_id={"rep": rep_at(2 * j)}, device_id_type=MESH)

    def sibling_copy(p, c, j, owner):
        block = gall.at[p, owner, :, piece(c)]
        return pltpu.make_async_remote_copy(
            src_ref=block, dst_ref=block,
            send_sem=ssend.at[p, c, j], recv_sem=srecv.at[p, c, j],
            device_id={"rep": sibling}, device_id_type=MESH)

    def make_grads(p, transposed, right):
        def one(k):
            at = pl.ds(pl.multiple_of(seg_at(k) * rows, rows), rows)
            return dot(transposed[at, :], right[...]).astype(BF16)

        def step(k):
            gsend[p, k] = one(k)

        loop(1, S, step)
        gall[p, rep, me] = one(0)

    def send(p, c):
        loop(1, S, lambda k: grad_copy(p, c, k, me).start())

    def sent(p, c):
        loop(1, S, lambda k: grad_copy(p, c, k, me).wait_send())

    send_after(UP, GATE)
    loop(1, S, lambda k: merged_copy(GATE, k, seg_from(k)).wait_recv())
    gate_s[...] = dot(x[...], mfull[GATE])
    send_after(DOWN, UP)
    loop(1, S, lambda k: merged_copy(UP, k, seg_from(k)).wait_recv())
    up_s[...] = dot(x[...], mfull[UP])
    CH = 32
    tokens = x.shape[0]

    def hidden(i):
        at = pl.ds(pl.multiple_of(i * CH, CH), CH)
        gate = gate_s[at, :]
        hid_s[at, :] = (gate * jax.nn.sigmoid(gate) * up_s[at, :]).astype(BF16)

    loop(0, tokens // CH, hidden)
    make_grads(DOWN, gt, hid_s)
    loop(1, S, lambda k: merged_copy(DOWN, k, me).wait_send())
    steps = [(p, c) for p in (DOWN, GATE, UP) for c in range(Q)]
    AHEAD = 2
    for p, c in steps[:AHEAD]:
        send(p, c)

    loop(1, S, lambda k: merged_copy(DOWN, k, seg_from(k)).wait_recv())
    dh_s[...] = dot(g[...], mfull[DOWN])

    def backward(i):
        at = pl.ds(pl.multiple_of(i * CH, CH), CH)
        gate = gate_s[at, :]
        dh = dh_s[at, :]
        sigma = jax.nn.sigmoid(gate)
        dgate_s[at, :] = (dh * up_s[at, :] * sigma * (1.0 + gate * (1.0 - sigma))).astype(BF16)
        dup_s[at, :] = (dh * (gate * sigma)).astype(BF16)

    loop(0, tokens // CH, backward)

    def input_grad(i):
        at = pl.ds(pl.multiple_of(i * rows, rows), rows)
        total = dot_t(dgate_s[...], mfull[GATE, at, :]) + dot_t(dup_s[...], mfull[UP, at, :])
        igv[:, at] = total.astype(BF16)

    ig_copy = pltpu.make_async_copy(igv, ig_hbm.at[0], out_sem.at[3])
    outs = (gg_hbm, gu_hbm, gd_hbm)
    out_copies = [ig_copy]
    for i in range(AHEAD, len(steps) + 4):
        if i < len(steps):
            sent(*steps[i - AHEAD])
            send(*steps[i])
        if i == AHEAD:
            make_grads(GATE, xt, dgate_s)
        if i == Q:
            make_grads(UP, xt, dup_s)
        if i == Q + 1:
            loop(0, S, input_grad)
            ig_copy.start()
        if i - 2 < len(steps):
            p, c = steps[i - 2]

            def arrived(k, p=p, c=c):
                grad_copy(p, c, k, seg_from(k)).wait_recv()

            loop(1, S, arrived)
            for j in range(1, chips):
                chip_copy(p, c, j, rep).start()
            sibling_copy(p, c, 0, rep).start()
        if 0 <= i - 3 < len(steps):
            p, c = steps[i - 3]
            for j in range(1, chips):
                chip_copy(p, c, j, rep_from(2 * j)).wait_recv()
                sibling_copy(p, c, j, rep_from(2 * j)).start()
        if 0 <= i - 4 < len(steps):
            p, c = steps[i - 4]
            for j in range(chips):
                sibling_copy(p, c, j, lax.rem(sibling - 2 * j + R, R)).wait_recv()

            def folded(b, p=p, c=c):
                at = pl.ds(pl.multiple_of(c * part + b * T, T), T)
                block = dot(fold[...], gall[p, :, :, at, :].reshape(R * S * T, H))
                outv[p, :, at, :] = block.astype(BF16).reshape(EL, T, H)

            loop(0, part // T, folded)
            if c == Q - 1:
                out = pltpu.make_async_copy(outv.at[p], outs[p], out_sem.at[p])
                out.start()
                out_copies.append(out)

    for k in range(1, R):
        coef_copy(k, rep).wait_send()
    for p, c in steps[-AHEAD:]:
        sent(p, c)
    for p, c in steps:
        for j in range(1, chips):
            chip_copy(p, c, j, rep).wait_send()
        for j in range(chips):
            sibling_copy(p, c, j, rep_from(2 * j)).wait_send()
    for out in out_copies:
        out.wait()


def place_kernel(n, *refs):
    sources, targets, held, sems = refs[:n], refs[n:2 * n], refs[2 * n:3 * n], refs[3 * n]
    loads = [pltpu.make_async_copy(a, b, sems.at[0, i]) for i, (a, b) in enumerate(zip(sources, held))]
    stores = [pltpu.make_async_copy(a, b, sems.at[1, i]) for i, (a, b) in enumerate(zip(held, targets))]
    for c in loads:
        c.start()
    for a, b in zip(loads, stores):
        a.wait()
        b.start()
    for c in stores:
        c.wait()


def place(arrays):
    n = len(arrays)
    any_spec = pl.BlockSpec(memory_space=pl.ANY)
    return pl.pallas_call(
        functools.partial(place_kernel, n),
        out_shape=tuple(jax.ShapeDtypeStruct(a.shape, a.dtype) for a in arrays),
        in_specs=[any_spec] * n,
        out_specs=(any_spec,) * n,
        scratch_shapes=[pltpu.VMEM(a.shape, a.dtype) for a in arrays] + [pltpu.SemaphoreType.DMA((2, n))],
        compiler_params=pltpu.CompilerParams(vmem_limit_bytes=58 * 1024 * 1024),
        cost_estimate=pl.CostEstimate(flops=0, bytes_accessed=4 * sum(a.size for a in arrays), transcendentals=0),
    )(*arrays)


def fused(S, R, tokens, cotangent, coefficients, w_gate, w_up, w_down):
    E, rows, H = w_gate.shape
    L, D = tokens.shape[1:]
    EL = E // R
    chips = R // 2
    lanes = -(-E // 128) * 128
    any_spec = pl.BlockSpec(memory_space=pl.ANY)
    dma = pltpu.SemaphoreType.DMA
    vmem = pltpu.VMEM
    grad = jax.ShapeDtypeStruct((EL, rows, H), BF16)
    flops = 16 * L * D * H + 2 * 3 * T * rows * H * E * S + 2 * 3 * T * rows * H * EL * R * S
    Q = 4
    made = pl.pallas_call(
        functools.partial(kernel, S, R),
        out_shape=(jax.ShapeDtypeStruct((1, L, D), BF16), grad, grad, grad),
        in_specs=[pl.BlockSpec(memory_space=vmem)] + [any_spec] * 5,
        out_specs=(any_spec,) * 4,
        scratch_shapes=[
            vmem((L, D), BF16), vmem((L, D), BF16), vmem((D, L), BF16), vmem((D, L), BF16),
            vmem((3, E, rows, H), BF16),
            vmem((3, S, rows, H), BF16),
            vmem((3, D, H), BF16),
            vmem((3, S, rows, H), BF16),
            vmem((3, R, S, rows, H), BF16),
            vmem((3, EL, rows, H), BF16),
            vmem((L, D), BF16),
            vmem((R, S, lanes), F32),
            vmem((S * T, E * T), BF16),
            vmem((EL * T, R * S * T), BF16),
            vmem((L, H), F32), vmem((L, H), F32), vmem((L, H), F32),
            vmem((L, H), BF16), vmem((L, H), BF16), vmem((L, H), BF16),
            dma((5,)), dma((4,)),
            dma((3, S)), dma((3, S)), dma((3, Q, S)), dma((3, Q, S)),
            dma((3, Q, chips)), dma((3, Q, chips)), dma((3, Q, chips)), dma((3, Q, chips)),
            dma((R,)), dma((R,)),
        ],
        compiler_params=pltpu.CompilerParams(
            collective_id=0, has_side_effects=True, vmem_limit_bytes=58 * 1024 * 1024),
        cost_estimate=pl.CostEstimate(
            flops=flops, bytes_accessed=2 * (3 * E * rows * H + 3 * L * D + 3 * EL * rows * H),
            transcendentals=2 * L * H),
    )(coefficients, tokens, cotangent, w_gate, w_up, w_down)
    return place(made)


def local(tokens, cotangent, coefficients, w_gate, w_up, w_down):
    mixing = coefficients[0]
    stacked = jnp.stack([w_gate, w_up, w_down])
    merged = jnp.einsum(
        "se,kedh->ksdh", mixing, stacked, preferred_element_type=jnp.float32
    ).astype(jnp.bfloat16)
    arrived = lax.all_to_all(merged, "seg", split_axis=1, concat_axis=2, tiled=True)
    merged_gate = arrived[0, 0]
    merged_up = arrived[1, 0]
    merged_down = arrived[2, 0]
    segment_x = tokens[0]
    segment_g = cotangent[0]
    contract = (((0,), (0,)), ((), ()))
    transposed = (((1,), (1,)), ((), ()))

    def fold_experts(pieces):
        return jnp.einsum("se,ksdh->kedh", mixing, pieces, preferred_element_type=jnp.float32)

    gate_proj = jnp.dot(segment_x, merged_gate, preferred_element_type=jnp.float32)
    up_proj = jnp.dot(segment_x, merged_up, preferred_element_type=jnp.float32)
    sigma = jax.nn.sigmoid(gate_proj)
    activated = gate_proj * sigma
    hidden = (activated * up_proj).astype(jnp.bfloat16)
    grad_down_seg = lax.dot_general(
        segment_g, hidden, contract, preferred_element_type=jnp.float32
    ).astype(jnp.bfloat16)
    down_folded = fold_experts(
        lax.all_to_all(grad_down_seg[None, None], "seg", split_axis=2, concat_axis=1, tiled=True)
    )
    down_summed = lax.psum_scatter(down_folded, "rep", scatter_dimension=1, tiled=True)
    d_hidden = jnp.dot(segment_g, merged_down, preferred_element_type=jnp.float32)
    d_gate = (d_hidden * up_proj * sigma * (1.0 + gate_proj * (1.0 - sigma))).astype(jnp.bfloat16)
    d_up = (d_hidden * activated).astype(jnp.bfloat16)
    input_grad = lax.dot_general(
        d_gate, merged_gate, transposed, preferred_element_type=jnp.float32
    )
    input_grad = input_grad + lax.dot_general(
        d_up, merged_up, transposed, preferred_element_type=jnp.float32
    )
    input_grad = input_grad.astype(jnp.bfloat16)
    grad_gate_seg = lax.dot_general(
        segment_x, d_gate, contract, preferred_element_type=jnp.float32
    ).astype(jnp.bfloat16)
    grad_up_seg = lax.dot_general(
        segment_x, d_up, contract, preferred_element_type=jnp.float32
    ).astype(jnp.bfloat16)
    pair = jnp.stack([grad_gate_seg, grad_up_seg])[:, None]
    pair_folded = fold_experts(lax.all_to_all(pair, "seg", split_axis=2, concat_axis=1, tiled=True))
    pair_summed = lax.psum_scatter(pair_folded, "rep", scatter_dimension=1, tiled=True)
    summed = jnp.concatenate([pair_summed, down_summed], axis=0)
    grads = summed.astype(jnp.bfloat16)
    return (input_grad[None], grads[0], grads[1], grads[2])


def solution(mesh):
    placed = (
        P("rep", "seg", None),
        P("rep", "seg", None),
        P("rep", None, None),
        P(None, "seg", None),
        P(None, "seg", None),
        P(None, "seg", None),
    )
    S, R = mesh.shape["seg"], mesh.shape["rep"]

    def body(tokens, cotangent, coefficients, w_gate, w_up, w_down):
        args = (tokens, cotangent, coefficients, w_gate, w_up, w_down)
        if w_gate.shape[1] % 128 == 0 and R % 2 == 0 and tokens.shape[1] % 128 == 0:
            return fused(S, R, *args)
        return local(*args)

    return jax.shard_map(
        body,
        mesh=mesh,
        in_specs=placed,
        out_specs=(
            P("rep", "seg", None),
            P("rep", "seg", None),
            P("rep", "seg", None),
            P("rep", "seg", None),
        ),
        check_vma=False,
    )
```

```python
import functools

import jax
import jax.numpy as jnp
from jax import lax
from jax.experimental import pallas as pl
from jax.experimental.pallas import tpu as pltpu
from jax.sharding import PartitionSpec as P

MESH = pl.DeviceIdType.MESH
F32 = jnp.float32
BF16 = jnp.bfloat16
T = 16
GATE, UP, DOWN = 0, 1, 2


def one_hot(shape, rows_of, columns_of):
    row = lax.broadcasted_iota(jnp.int32, shape, 0)
    column = lax.broadcasted_iota(jnp.int32, shape, 1)
    return rows_of(row) == columns_of(column)


def dot(a, b):
    return jnp.dot(a, b, preferred_element_type=F32)


def dot_t(a, b):
    return lax.dot_general(a, b, (((1,), (1,)), ((), ())), preferred_element_type=F32)


def kernel(
    S, R, Q, coef_ref, tok_hbm, cot_hbm, wg_hbm, wu_hbm, wd_hbm,
    ig_hbm, gg_hbm, gu_hbm, gd_hbm,
    x, g, xt, gt, xp, gp, xpt, gpt, w, msend, mfull, mdown, gown, ghelp, gall, outv, igv, cbuf, mix, fold,
    gate_s, up_s, dh_s, dhp_s, dhr, d_s, dr,
    load_sem, out_sem, fsend, frecv, dsend, drecv, psend, precv,
    osend, orecv, hsend, hrecv, xsend, xrecv, ssend, srecv, csend, crecv,
):
    me = lax.axis_index("seg")
    rep = lax.axis_index("rep")
    E, rows, H = w.shape[1:]
    EL = outv.shape[1]
    L = x.shape[0]
    chips = R // 2
    sibling = rep + 1 - 2 * lax.rem(rep, 2)
    HS = S // 2
    place = lax.rem(me, HS)
    base = me - place
    other = HS - base
    partner = other + place

    def seg_at(k):
        return lax.rem(me + k, S)

    def seg_from(k):
        return lax.rem(me - k + S, S)

    def place_at(k):
        return lax.rem(place + k, HS)

    def place_from(k):
        return lax.rem(place - k + HS, HS)

    def rep_at(k):
        return lax.rem(rep + k, R)

    def rep_from(k):
        return lax.rem(rep - k + R, R)

    def loop(lo, hi, body):
        lax.fori_loop(lo, hi, lambda i, c: (body(i), c)[1], 0)

    def span(start, count=1):
        return pl.ds(pl.multiple_of(start * rows, rows), count * rows)

    loads = [pltpu.make_async_copy(tok_hbm.at[0], x, load_sem.at[0]),
             pltpu.make_async_copy(cot_hbm.at[0], g, load_sem.at[1])]
    w_loads = [pltpu.make_async_copy(h, w.at[p], load_sem.at[2 + p])
               for p, h in enumerate((wg_hbm, wu_hbm, wd_hbm))]
    for c in w_loads + loads:
        c.start()

    barrier = pltpu.get_barrier_semaphore()
    for k in range(1, S):
        pl.semaphore_signal(barrier, inc=1, device_id={"seg": seg_at(k)}, device_id_type=MESH)
    for k in range(1, R):
        pl.semaphore_signal(barrier, inc=1, device_id={"rep": rep_at(k)}, device_id_type=MESH)

    coef = coef_ref[0].astype(F32)
    LANES = cbuf.shape[2]
    cbuf[rep] = dot(coef, one_hot((E, LANES), lambda i: i, lambda j: j).astype(F32))
    tall = dot(one_hot((S * T, S), lambda i: i // T, lambda j: j).astype(F32), coef)
    wide = dot(tall, one_hot((E, E * T), lambda i: i, lambda j: j // T).astype(F32))
    keep = one_hot((S * T, E * T), lambda i: i % T, lambda j: j % T)
    mix[...] = jnp.where(keep, wide, 0.0).astype(BF16)

    pl.semaphore_wait(barrier, S - 1 + R - 1)

    def coef_copy(k, owner):
        return pltpu.make_async_remote_copy(
            src_ref=cbuf.at[owner], dst_ref=cbuf.at[owner],
            send_sem=csend.at[k], recv_sem=crecv.at[k],
            device_id={"rep": rep_at(k)}, device_id_type=MESH)

    for k in range(1, R):
        coef_copy(k, rep).start()

    def merged_copy(p, k, owner):
        return pltpu.make_async_remote_copy(
            src_ref=msend.at[p, seg_at(k)], dst_ref=mfull.at[p, span(owner)],
            send_sem=fsend.at[p, k], recv_sem=frecv.at[p, k],
            device_id={"seg": seg_at(k)}, device_id_type=MESH)

    def down_copy(t, k, owner):
        to = place_at(k)
        return pltpu.make_async_remote_copy(
            src_ref=msend.at[DOWN, (base if t == 0 else other) + to], dst_ref=mdown.at[t, span(owner)],
            send_sem=dsend.at[t, k], recv_sem=drecv.at[t, k],
            device_id={"seg": base + to}, device_id_type=MESH)

    def to_partner(n, source, target):
        return pltpu.make_async_remote_copy(
            src_ref=source, dst_ref=target, send_sem=psend.at[n], recv_sem=precv.at[n],
            device_id={"seg": partner}, device_id_type=MESH)

    x_out = to_partner(0, x.at[:, span(other, HS)], xp)
    g_out = to_partner(1, g.at[:, span(other, HS)], gp)
    dh_out = to_partner(2, dhp_s, dhr)
    d_out = [to_partner(3 + p, d_s.at[p], dr.at[p]) for p in (GATE, UP, DOWN)]

    for p in (GATE, UP, DOWN):
        w_loads[p].wait()

        def merge(b, p=p):
            at = pl.ds(pl.multiple_of(b * T, T), T)
            block = dot(mix[...], w[p, :, at, :].reshape(E * T, H))
            msend[p, :, at, :] = block.astype(BF16).reshape(S, T, H)

        loop(0, rows // T, merge)
        if p == GATE:
            loop(1, S, lambda k: merged_copy(GATE, k, me).start())
        if p == DOWN:
            for k in range(1, HS):
                for t in range(2):
                    down_copy(t, k, place).start()
            mdown[0, span(place), :] = msend[DOWN, me]
            mdown[1, span(place), :] = msend[DOWN, partner]
        else:
            mfull[p, span(me), :] = msend[p, me]

    for c in loads:
        c.wait()
    xt[...] = x[:, span(base, HS)].T
    gt[...] = g[:, span(base, HS)].T
    for k in range(1, R):
        coef_copy(k, rep_from(k)).wait_recv()
    every = cbuf[...].reshape(R * S, LANES)
    mine = one_hot((EL * T, LANES), lambda i: i // T + rep * EL, lambda j: j).astype(F32)
    tall = dot_t(mine, every)
    wide = dot(tall, one_hot((R * S, R * S * T), lambda i: i, lambda j: j // T).astype(F32))
    keep = one_hot((EL * T, R * S * T), lambda i: i % T, lambda j: j % T)
    fold[...] = jnp.where(keep, wide, 0.0).astype(BF16)

    part = rows // Q

    def piece(c):
        return pl.ds(c * part, part)

    def own_copy(p, k, owner):
        return pltpu.make_async_remote_copy(
            src_ref=gown.at[p, k], dst_ref=gall.at[p, rep, base + owner],
            send_sem=osend.at[p, k], recv_sem=orecv.at[p, k],
            device_id={"seg": base + place_at(k)}, device_id_type=MESH)

    def help_copy(p, c, k, owner):
        return pltpu.make_async_remote_copy(
            src_ref=ghelp.at[p, k, piece(c)], dst_ref=gall.at[p, rep, other + owner, piece(c)],
            send_sem=hsend.at[p, c, k], recv_sem=hrecv.at[p, c, k],
            device_id={"seg": base + place_at(k)}, device_id_type=MESH)

    def unit(p, c, owner):
        if c == Q:
            return gall.at[p, owner, pl.ds(base, HS)]
        return gall.at[p, owner, pl.ds(other, HS), piece(c)]

    def chip_copy(p, c, j, owner):
        block = unit(p, c, owner)
        return pltpu.make_async_remote_copy(
            src_ref=block, dst_ref=block,
            send_sem=xsend.at[p, c, j], recv_sem=xrecv.at[p, c, j],
            device_id={"rep": rep_at(2 * j)}, device_id_type=MESH)

    def sibling_copy(p, c, j, owner):
        block = unit(p, c, owner)
        return pltpu.make_async_remote_copy(
            src_ref=block, dst_ref=block,
            send_sem=ssend.at[p, c, j], recv_sem=srecv.at[p, c, j],
            device_id={"rep": sibling}, device_id_type=MESH)

    def make_own(p):
        transposed = gt if p == DOWN else xt

        def one(k):
            return dot(transposed[span(place_at(k)), :], d_s[p]).astype(BF16)

        def step(k):
            gown[p, k] = one(k)
            own_copy(p, k, place).start()

        loop(1, HS, step)
        gall[p, rep, me] = one(0)

    def make_help(p):
        transposed = gpt if p == DOWN else xpt

        def one(k):
            return dot(transposed[span(place_at(k)), :], dr[p]).astype(BF16)

        def step(k):
            ghelp[p, k] = one(k)

        loop(1, HS, step)
        gall[p, rep, partner] = one(0)
        for c in range(Q):
            loop(1, HS, lambda k, c=c: help_copy(p, c, k, place).start())

    def pass_on(p, c):
        def arrived(k):
            if c == Q:
                own_copy(p, k, place_from(k)).wait_recv()
            else:
                help_copy(p, c, k, place_from(k)).wait_recv()

        loop(1, HS, arrived)
        for j in range(1, chips):
            chip_copy(p, c, j, rep).start()
        sibling_copy(p, c, 0, rep).start()

    def hand_over(p, c):
        for j in range(1, chips):
            chip_copy(p, c, j, rep_from(2 * j)).wait_recv()
            sibling_copy(p, c, j, rep_from(2 * j)).start()

    def collect(p, c):
        for j in range(chips):
            sibling_copy(p, c, j, lax.rem(sibling - 2 * j + R, R)).wait_recv()

    def fold_piece(p, c):
        collect(p, c)

        def folded(b):
            at = pl.ds(pl.multiple_of(c * part + b * T, T), T)
            block = dot(fold[...], gall[p, :, :, at, :].reshape(R * S * T, H))
            outv[p, :, at, :] = block.astype(BF16).reshape(EL, T, H)

        loop(0, part // T, folded)

    outs = (gg_hbm, gu_hbm, gd_hbm)
    out_copies = [pltpu.make_async_copy(outv.at[p], outs[p], out_sem.at[p]) for p in (GATE, UP, DOWN)]
    ig_copy = pltpu.make_async_copy(igv, ig_hbm.at[0], out_sem.at[3])

    def send_up(k):
        merged_copy(GATE, k, me).wait_send()
        merged_copy(UP, k, me).start()

    loop(1, S, send_up)
    g_out.start()
    loop(1, S, lambda k: merged_copy(GATE, k, seg_from(k)).wait_recv())
    gate_s[...] = dot(x[...], mfull[GATE])
    for k in range(1, HS):
        for t in range(2):
            down_copy(t, k, place_from(k)).wait_recv()
    dh_s[...] = dot(g[:, span(base, HS)], mdown[0])

    loop(1, S, lambda k: merged_copy(UP, k, seg_from(k)).wait_recv())
    up_s[...] = dot(x[...], mfull[UP])
    CH = 32

    def chunk(i):
        return pl.ds(pl.multiple_of(i * CH, CH), CH)

    def hidden(i):
        at = chunk(i)
        gate = gate_s[at, :]
        d_s[DOWN, at, :] = (gate * jax.nn.sigmoid(gate) * up_s[at, :]).astype(BF16)

    loop(0, L // CH, hidden)
    d_out[DOWN].start()
    make_own(DOWN)
    g_out.wait_recv()
    dhp_s[...] = dot(gp[...], mdown[1]).astype(BF16)
    dh_out.start()
    gpt[...] = gp[...].T
    x_out.start()
    pass_on(DOWN, Q)
    d_out[DOWN].wait_recv()
    make_help(DOWN)

    dh_out.wait_recv()

    def backward(i):
        at = chunk(i)
        gate = gate_s[at, :]
        dh = dh_s[at, :] + dhr[at, :].astype(F32)
        sigma = jax.nn.sigmoid(gate)
        d_s[GATE, at, :] = (dh * up_s[at, :] * sigma * (1.0 + gate * (1.0 - sigma))).astype(BF16)
        d_s[UP, at, :] = (dh * (gate * sigma)).astype(BF16)

    loop(0, L // CH, backward)
    d_out[GATE].start()
    make_own(GATE)
    make_own(UP)
    for c in range(Q):
        pass_on(DOWN, c)
    x_out.wait_recv()
    xpt[...] = xp[...].T
    d_out[GATE].wait_send()
    d_out[UP].start()
    pass_on(GATE, Q)
    hand_over(DOWN, Q)

    def input_grad(i):
        at = span(i)
        total = dot_t(d_s[GATE], mfull[GATE, at, :]) + dot_t(d_s[UP], mfull[UP, at, :])
        igv[:, at] = total.astype(BF16)

    loop(0, S, input_grad)
    ig_copy.start()
    pass_on(UP, Q)
    d_out[GATE].wait_recv()
    make_help(GATE)
    collect(DOWN, Q)
    for c in range(Q):
        hand_over(DOWN, c)
    for c in range(Q):
        pass_on(GATE, c)
    for c in range(Q):
        fold_piece(DOWN, c)
    out_copies[DOWN].start()
    d_out[UP].wait_recv()
    make_help(UP)
    hand_over(GATE, Q)
    hand_over(UP, Q)
    for c in range(Q):
        pass_on(UP, c)
    for p in (GATE, UP):
        collect(p, Q)
        for c in range(Q + 1):
            if c < Q:
                hand_over(p, c)
            if c > 0:
                fold_piece(p, c - 1)
        out_copies[p].start()

    for k in range(1, R):
        coef_copy(k, rep).wait_send()
    loop(1, S, lambda k: merged_copy(UP, k, me).wait_send())
    for c in (x_out, g_out, dh_out, d_out[UP], d_out[DOWN]):
        c.wait_send()
    for k in range(1, HS):
        for t in range(2):
            down_copy(t, k, place).wait_send()
    for p in (GATE, UP, DOWN):
        loop(1, HS, lambda k, p=p: own_copy(p, k, place).wait_send())
        for c in range(Q):
            loop(1, HS, lambda k, p=p, c=c: help_copy(p, c, k, place).wait_send())
        for c in range(Q + 1):
            for j in range(1, chips):
                chip_copy(p, c, j, rep).wait_send()
            for j in range(chips):
                sibling_copy(p, c, j, rep_from(2 * j)).wait_send()
    ig_copy.wait()
    for c in out_copies:
        c.wait()


def place_kernel(n, *refs):
    sources, targets, held, sems = refs[:n], refs[n:2 * n], refs[2 * n:3 * n], refs[3 * n]
    loads = [pltpu.make_async_copy(a, b, sems.at[0, i]) for i, (a, b) in enumerate(zip(sources, held))]
    stores = [pltpu.make_async_copy(a, b, sems.at[1, i]) for i, (a, b) in enumerate(zip(held, targets))]
    for c in loads:
        c.start()
    for a, b in zip(loads, stores):
        a.wait()
        b.start()
    for c in stores:
        c.wait()


def place(arrays):
    n = len(arrays)
    any_spec = pl.BlockSpec(memory_space=pl.ANY)
    return pl.pallas_call(
        functools.partial(place_kernel, n),
        out_shape=tuple(jax.ShapeDtypeStruct(a.shape, a.dtype) for a in arrays),
        in_specs=[any_spec] * n,
        out_specs=(any_spec,) * n,
        scratch_shapes=[pltpu.VMEM(a.shape, a.dtype) for a in arrays] + [pltpu.SemaphoreType.DMA((2, n))],
        compiler_params=pltpu.CompilerParams(vmem_limit_bytes=58 * 1024 * 1024),
        cost_estimate=pl.CostEstimate(flops=0, bytes_accessed=4 * sum(a.size for a in arrays), transcendentals=0),
    )(*arrays)


def fused(S, R, tokens, cotangent, coefficients, w_gate, w_up, w_down):
    E, rows, H = w_gate.shape
    L, D = tokens.shape[1:]
    EL = E // R
    chips = R // 2
    lanes = -(-E // 128) * 128
    any_spec = pl.BlockSpec(memory_space=pl.ANY)
    dma = pltpu.SemaphoreType.DMA
    vmem = pltpu.VMEM
    grad = jax.ShapeDtypeStruct((EL, rows, H), BF16)
    flops = 16 * L * D * H + 2 * 3 * T * rows * H * E * S + 2 * 3 * T * rows * H * EL * R * S
    Q = 4
    made = pl.pallas_call(
        functools.partial(kernel, S, R, Q),
        out_shape=(jax.ShapeDtypeStruct((1, L, D), BF16), grad, grad, grad),
        in_specs=[pl.BlockSpec(memory_space=vmem)] + [any_spec] * 5,
        out_specs=(any_spec,) * 4,
        scratch_shapes=[
            vmem((L, D), BF16), vmem((L, D), BF16), vmem((D // 2, L), BF16), vmem((D // 2, L), BF16),
            vmem((L, D // 2), BF16), vmem((L, D // 2), BF16), vmem((D // 2, L), BF16), vmem((D // 2, L), BF16),
            vmem((3, E, rows, H), BF16),
            vmem((3, S, rows, H), BF16),
            vmem((2, D, H), BF16),
            vmem((2, D // 2, H), BF16),
            vmem((3, S // 2, rows, H), BF16), vmem((3, S // 2, rows, H), BF16),
            vmem((3, R, S, rows, H), BF16),
            vmem((3, EL, rows, H), BF16),
            vmem((L, D), BF16),
            vmem((R, S, lanes), F32),
            vmem((S * T, E * T), BF16),
            vmem((EL * T, R * S * T), BF16),
            vmem((L, H), F32), vmem((L, H), F32), vmem((L, H), F32),
            vmem((L, H), BF16), vmem((L, H), BF16),
            vmem((3, L, H), BF16), vmem((3, L, H), BF16),
            dma((5,)), dma((4,)),
            dma((2, S)), dma((2, S)), dma((2, S // 2)), dma((2, S // 2)),
            dma((6,)), dma((6,)),
            dma((3, S // 2)), dma((3, S // 2)), dma((3, Q, S // 2)), dma((3, Q, S // 2)),
            dma((3, Q + 1, chips)), dma((3, Q + 1, chips)), dma((3, Q + 1, chips)), dma((3, Q + 1, chips)),
            dma((R,)), dma((R,)),
        ],
        compiler_params=pltpu.CompilerParams(
            collective_id=0, has_side_effects=True, vmem_limit_bytes=58 * 1024 * 1024),
        cost_estimate=pl.CostEstimate(
            flops=flops, bytes_accessed=2 * (3 * E * rows * H + 3 * L * D + 3 * EL * rows * H),
            transcendentals=2 * L * H),
    )(coefficients, tokens, cotangent, w_gate, w_up, w_down)
    return place(made)


def local(tokens, cotangent, coefficients, w_gate, w_up, w_down):
    mixing = coefficients[0]
    stacked = jnp.stack([w_gate, w_up, w_down])
    merged = jnp.einsum(
        "se,kedh->ksdh", mixing, stacked, preferred_element_type=jnp.float32
    ).astype(jnp.bfloat16)
    arrived = lax.all_to_all(merged, "seg", split_axis=1, concat_axis=2, tiled=True)
    merged_gate = arrived[0, 0]
    merged_up = arrived[1, 0]
    merged_down = arrived[2, 0]
    segment_x = tokens[0]
    segment_g = cotangent[0]
    contract = (((0,), (0,)), ((), ()))
    transposed = (((1,), (1,)), ((), ()))

    def fold_experts(pieces):
        return jnp.einsum("se,ksdh->kedh", mixing, pieces, preferred_element_type=jnp.float32)

    gate_proj = jnp.dot(segment_x, merged_gate, preferred_element_type=jnp.float32)
    up_proj = jnp.dot(segment_x, merged_up, preferred_element_type=jnp.float32)
    sigma = jax.nn.sigmoid(gate_proj)
    activated = gate_proj * sigma
    hidden = (activated * up_proj).astype(jnp.bfloat16)
    grad_down_seg = lax.dot_general(
        segment_g, hidden, contract, preferred_element_type=jnp.float32
    ).astype(jnp.bfloat16)
    down_folded = fold_experts(
        lax.all_to_all(grad_down_seg[None, None], "seg", split_axis=2, concat_axis=1, tiled=True)
    )
    down_summed = lax.psum_scatter(down_folded, "rep", scatter_dimension=1, tiled=True)
    d_hidden = jnp.dot(segment_g, merged_down, preferred_element_type=jnp.float32)
    d_gate = (d_hidden * up_proj * sigma * (1.0 + gate_proj * (1.0 - sigma))).astype(jnp.bfloat16)
    d_up = (d_hidden * activated).astype(jnp.bfloat16)
    input_grad = lax.dot_general(
        d_gate, merged_gate, transposed, preferred_element_type=jnp.float32
    )
    input_grad = input_grad + lax.dot_general(
        d_up, merged_up, transposed, preferred_element_type=jnp.float32
    )
    input_grad = input_grad.astype(jnp.bfloat16)
    grad_gate_seg = lax.dot_general(
        segment_x, d_gate, contract, preferred_element_type=jnp.float32
    ).astype(jnp.bfloat16)
    grad_up_seg = lax.dot_general(
        segment_x, d_up, contract, preferred_element_type=jnp.float32
    ).astype(jnp.bfloat16)
    pair = jnp.stack([grad_gate_seg, grad_up_seg])[:, None]
    pair_folded = fold_experts(lax.all_to_all(pair, "seg", split_axis=2, concat_axis=1, tiled=True))
    pair_summed = lax.psum_scatter(pair_folded, "rep", scatter_dimension=1, tiled=True)
    summed = jnp.concatenate([pair_summed, down_summed], axis=0)
    grads = summed.astype(jnp.bfloat16)
    return (input_grad[None], grads[0], grads[1], grads[2])


def solution(mesh):
    placed = (
        P("rep", "seg", None),
        P("rep", "seg", None),
        P("rep", None, None),
        P(None, "seg", None),
        P(None, "seg", None),
        P(None, "seg", None),
    )
    S, R = mesh.shape["seg"], mesh.shape["rep"]

    def body(tokens, cotangent, coefficients, w_gate, w_up, w_down):
        args = (tokens, cotangent, coefficients, w_gate, w_up, w_down)
        if w_gate.shape[1] % 128 == 0 and R % 2 == 0 and S % 2 == 0 and tokens.shape[1] % 128 == 0:
            return fused(S, R, *args)
        return local(*args)

    return jax.shard_map(
        body,
        mesh=mesh,
        in_specs=placed,
        out_specs=(
            P("rep", "seg", None),
            P("rep", "seg", None),
            P("rep", "seg", None),
            P("rep", "seg", None),
        ),
        check_vma=False,
    )
```

```python
import functools

import jax
import jax.numpy as jnp
from jax import lax
from jax.experimental import pallas as pl
from jax.experimental.pallas import tpu as pltpu
from jax.sharding import PartitionSpec as P

MESH = pl.DeviceIdType.MESH
F32 = jnp.float32
BF16 = jnp.bfloat16
T = 16
GATE, UP, DOWN = 0, 1, 2
PIECES = {GATE: 2, UP: 4, DOWN: 2}
MOST = max(PIECES.values())
HEAD = 32


def one_hot(shape, rows_of, columns_of):
    row = lax.broadcasted_iota(jnp.int32, shape, 0)
    column = lax.broadcasted_iota(jnp.int32, shape, 1)
    return rows_of(row) == columns_of(column)


def dot(a, b):
    return jnp.dot(a, b, preferred_element_type=F32)


def dot_t(a, b):
    return lax.dot_general(a, b, (((1,), (1,)), ((), ())), preferred_element_type=F32)


def kernel(
    S, R, coef_ref, tok_hbm, cot_hbm, wg_hbm, wu_hbm, wd_hbm,
    ig_hbm, gg_hbm, gu_hbm, gd_hbm,
    x, g, xt, gt, xp, gp, xpt, gpt, w, msend, mfull, mdown, gown, ghelp, gall, outv, igv, cbuf, mix, fold,
    gate_s, up_s, dh_s, dhp_s, dhr, d_s, dr,
    load_sem, out_sem, fsend, frecv, dsend, drecv, psend, precv,
    osend, orecv, hsend, hrecv, xsend, xrecv, ssend, srecv, csend, crecv,
):
    me = lax.axis_index("seg")
    rep = lax.axis_index("rep")
    E, rows, H = w.shape[1:]
    EL = outv.shape[1]
    L = x.shape[0]
    chips = R // 2
    sibling = rep + 1 - 2 * lax.rem(rep, 2)
    HS = S // 2
    place = lax.rem(me, HS)
    base = me - place
    other = HS - base
    partner = other + place

    def seg_at(k):
        return lax.rem(me + k, S)

    def seg_from(k):
        return lax.rem(me - k + S, S)

    def place_at(k):
        return lax.rem(place + k, HS)

    def place_from(k):
        return lax.rem(place - k + HS, HS)

    def rep_at(k):
        return lax.rem(rep + k, R)

    def rep_from(k):
        return lax.rem(rep - k + R, R)

    def loop(lo, hi, body):
        lax.fori_loop(lo, hi, lambda i, c: (body(i), c)[1], 0)

    def span(start, count=1):
        return pl.ds(pl.multiple_of(start * rows, rows), count * rows)

    loads = [pltpu.make_async_copy(tok_hbm.at[0], x, load_sem.at[0]),
             pltpu.make_async_copy(cot_hbm.at[0], g, load_sem.at[1])]
    w_loads = {p: pltpu.make_async_copy(h, w.at[p], load_sem.at[1 + p])
               for p, h in ((UP, wu_hbm), (DOWN, wd_hbm))}

    def head(n):
        return pl.ds(n * HEAD, HEAD)

    heads = [pltpu.make_async_copy(wg_hbm.at[:, head(n), :], w.at[GATE, :, head(n), :], load_sem.at[4 + n])
             for n in range(rows // HEAD)]
    for c in heads:
        c.start()

    barrier = pltpu.get_barrier_semaphore()
    for k in range(1, S):
        pl.semaphore_signal(barrier, inc=1, device_id={"seg": seg_at(k)}, device_id_type=MESH)
    for k in range(1, R):
        pl.semaphore_signal(barrier, inc=1, device_id={"rep": rep_at(k)}, device_id_type=MESH)

    coef = coef_ref[0].astype(F32)
    LANES = cbuf.shape[2]
    cbuf[rep] = dot(coef, one_hot((E, LANES), lambda i: i, lambda j: j).astype(F32))
    tall = dot(one_hot((S * T, S), lambda i: i // T, lambda j: j).astype(F32), coef)
    wide = dot(tall, one_hot((E, E * T), lambda i: i, lambda j: j // T).astype(F32))
    keep = one_hot((S * T, E * T), lambda i: i % T, lambda j: j % T)
    mix[...] = jnp.where(keep, wide, 0.0).astype(BF16)

    pl.semaphore_wait(barrier, S - 1 + R - 1)

    def coef_copy(k, owner):
        return pltpu.make_async_remote_copy(
            src_ref=cbuf.at[owner], dst_ref=cbuf.at[owner],
            send_sem=csend.at[k], recv_sem=crecv.at[k],
            device_id={"rep": rep_at(k)}, device_id_type=MESH)

    for k in range(1, R):
        coef_copy(k, rep).start()

    def merged_copy(p, k, owner):
        return pltpu.make_async_remote_copy(
            src_ref=msend.at[p, seg_at(k)], dst_ref=mfull.at[p, span(owner)],
            send_sem=fsend.at[p, k], recv_sem=frecv.at[p, k],
            device_id={"seg": seg_at(k)}, device_id_type=MESH)

    def down_copy(t, k, owner):
        to = place_at(k)
        return pltpu.make_async_remote_copy(
            src_ref=msend.at[DOWN, (base if t == 0 else other) + to], dst_ref=mdown.at[t, span(owner)],
            send_sem=dsend.at[t, k], recv_sem=drecv.at[t, k],
            device_id={"seg": base + to}, device_id_type=MESH)

    def to_partner(n, source, target):
        return pltpu.make_async_remote_copy(
            src_ref=source, dst_ref=target, send_sem=psend.at[n], recv_sem=precv.at[n],
            device_id={"seg": partner}, device_id_type=MESH)

    x_out = to_partner(0, x.at[:, span(other, HS)], xp)
    g_out = to_partner(1, g.at[:, span(other, HS)], gp)
    dh_out = to_partner(2, dhp_s, dhr)

    def columns(p, c):
        width = H // PIECES[p]
        return pl.ds(c * width, width)

    d_out = [[to_partner(3 + p * MOST + c, d_s.at[p, :, columns(p, c)], dr.at[p, :, columns(p, c)])
              for c in range(PIECES[p])] for p in (GATE, UP, DOWN)]

    def merge(p, b):
        at = pl.ds(pl.multiple_of(b * T, T), T)
        block = dot(mix[...], w[p, :, at, :].reshape(E * T, H))
        msend[p, :, at, :] = block.astype(BF16).reshape(S, T, H)

    for n, c in enumerate(heads):
        c.wait()
        loop(n * HEAD // T, (n + 1) * HEAD // T, lambda b: merge(GATE, b))

        def send_head(k, n=n):
            pltpu.make_async_remote_copy(
                src_ref=msend.at[GATE, seg_at(k), head(n)],
                dst_ref=mfull.at[GATE, pl.ds(pl.multiple_of(me * rows, rows) + n * HEAD, HEAD)],
                send_sem=fsend.at[GATE, k], recv_sem=frecv.at[GATE, k],
                device_id={"seg": seg_at(k)}, device_id_type=MESH).start()

        loop(1, S, send_head)
        if n == 0:
            for c in list(w_loads.values()) + loads:
                c.start()
    mfull[GATE, span(me), :] = msend[GATE, me]
    w_loads[UP].wait()
    loop(0, rows // T, lambda b: merge(UP, b))
    mfull[UP, span(me), :] = msend[UP, me]
    w_loads[DOWN].wait()
    loop(0, rows // T, lambda b: merge(DOWN, b))
    for k in range(1, HS):
        for t in range(2):
            down_copy(t, k, place).start()
    mdown[0, span(place), :] = msend[DOWN, me]
    mdown[1, span(place), :] = msend[DOWN, partner]

    for c in loads:
        c.wait()
    xt[...] = x[:, span(base, HS)].T
    gt[...] = g[:, span(base, HS)].T
    for k in range(1, R):
        coef_copy(k, rep_from(k)).wait_recv()
    every = cbuf[...].reshape(R * S, LANES)
    mine = one_hot((EL * T, LANES), lambda i: i // T + rep * EL, lambda j: j).astype(F32)
    tall = dot_t(mine, every)
    wide = dot(tall, one_hot((R * S, R * S * T), lambda i: i, lambda j: j // T).astype(F32))
    keep = one_hot((EL * T, R * S * T), lambda i: i % T, lambda j: j % T)
    fold[...] = jnp.where(keep, wide, 0.0).astype(BF16)

    WHOLE = MOST

    def own_copy(p, k, owner):
        return pltpu.make_async_remote_copy(
            src_ref=gown.at[p, k], dst_ref=gall.at[p, rep, base + owner],
            send_sem=osend.at[p, k], recv_sem=orecv.at[p, k],
            device_id={"seg": base + place_at(k)}, device_id_type=MESH)

    def help_copy(p, c, k, owner):
        return pltpu.make_async_remote_copy(
            src_ref=ghelp.at[p, k, :, columns(p, c)],
            dst_ref=gall.at[p, rep, other + owner, :, columns(p, c)],
            send_sem=hsend.at[p, c, k], recv_sem=hrecv.at[p, c, k],
            device_id={"seg": base + place_at(k)}, device_id_type=MESH)

    def unit(p, c, owner):
        if c == WHOLE:
            return gall.at[p, owner, pl.ds(base, HS)]
        return gall.at[p, owner, pl.ds(other, HS), :, columns(p, c)]

    def chip_copy(p, c, j, owner):
        block = unit(p, c, owner)
        return pltpu.make_async_remote_copy(
            src_ref=block, dst_ref=block,
            send_sem=xsend.at[p, c, j], recv_sem=xrecv.at[p, c, j],
            device_id={"rep": rep_at(2 * j)}, device_id_type=MESH)

    def sibling_copy(p, c, j, owner):
        block = unit(p, c, owner)
        return pltpu.make_async_remote_copy(
            src_ref=block, dst_ref=block,
            send_sem=ssend.at[p, c, j], recv_sem=srecv.at[p, c, j],
            device_id={"rep": sibling}, device_id_type=MESH)

    def make_own(p):
        transposed = gt if p == DOWN else xt

        def one(k):
            return dot(transposed[span(place_at(k)), :], d_s[p]).astype(BF16)

        def step(k):
            gown[p, k] = one(k)
            own_copy(p, k, place).start()

        loop(1, HS, step)
        gall[p, rep, me] = one(0)

    def make_help(p, c):
        d_out[p][c].wait_recv()
        transposed = gpt if p == DOWN else xpt

        def one(k):
            return dot(transposed[span(place_at(k)), :], dr[p, :, columns(p, c)]).astype(BF16)

        def step(k):
            ghelp[p, k, :, columns(p, c)] = one(k)
            help_copy(p, c, k, place).start()

        loop(1, HS, step)
        gall[p, rep, partner, :, columns(p, c)] = one(0)

    def pass_on(p, c):
        def arrived(k):
            if c == WHOLE:
                own_copy(p, k, place_from(k)).wait_recv()
            else:
                help_copy(p, c, k, place_from(k)).wait_recv()

        loop(1, HS, arrived)
        for j in range(1, chips):
            chip_copy(p, c, j, rep).start()
        sibling_copy(p, c, 0, rep).start()

    def hand_over(p, c):
        for j in range(1, chips):
            chip_copy(p, c, j, rep_from(2 * j)).wait_recv()
            sibling_copy(p, c, j, rep_from(2 * j)).start()

    def collect(p, c):
        for j in range(chips):
            sibling_copy(p, c, j, lax.rem(sibling - 2 * j + R, R)).wait_recv()

    def fold_piece(p, c):
        collect(p, c)

        def folded(b):
            at = pl.ds(pl.multiple_of(b * T, T), T)
            width = H // PIECES[p]
            block = dot(fold[...], gall[p, :, :, at, columns(p, c)].reshape(R * S * T, width))
            outv[p, :, at, columns(p, c)] = block.astype(BF16).reshape(EL, T, width)

        loop(0, rows // T, folded)

    outs = (gg_hbm, gu_hbm, gd_hbm)
    out_copies = [pltpu.make_async_copy(outv.at[p], outs[p], out_sem.at[p]) for p in (GATE, UP, DOWN)]
    ig_copy = pltpu.make_async_copy(igv, ig_hbm.at[0], out_sem.at[3])

    def send_up(k):
        merged_copy(GATE, k, me).wait_send()
        merged_copy(UP, k, me).start()

    loop(1, S, send_up)
    g_out.start()
    loop(1, S, lambda k: merged_copy(GATE, k, seg_from(k)).wait_recv())
    gate_s[...] = dot(x[...], mfull[GATE])
    for k in range(1, HS):
        for t in range(2):
            down_copy(t, k, place_from(k)).wait_recv()
    dh_s[...] = dot(g[:, span(base, HS)], mdown[0])

    loop(1, S, lambda k: merged_copy(UP, k, seg_from(k)).wait_recv())
    up_s[...] = dot(x[...], mfull[UP])
    CH = 32

    def chunk(i):
        return pl.ds(pl.multiple_of(i * CH, CH), CH)

    def hidden(i):
        at = chunk(i)
        gate = gate_s[at, :]
        d_s[DOWN, at, :] = (gate * jax.nn.sigmoid(gate) * up_s[at, :]).astype(BF16)

    loop(0, L // CH, hidden)
    for c in d_out[DOWN]:
        c.start()
    make_own(DOWN)
    g_out.wait_recv()
    dhp_s[...] = dot(gp[...], mdown[1]).astype(BF16)
    dh_out.start()
    gpt[...] = gp[...].T
    x_out.start()
    pass_on(DOWN, WHOLE)
    for c in range(PIECES[DOWN]):
        make_help(DOWN, c)
    hand_over(DOWN, WHOLE)
    for c in range(PIECES[DOWN]):
        pass_on(DOWN, c)
    dh_out.wait_recv()

    def backward(i):
        at = chunk(i)
        gate = gate_s[at, :]
        dh = dh_s[at, :] + dhr[at, :].astype(F32)
        sigma = jax.nn.sigmoid(gate)
        d_s[GATE, at, :] = (dh * up_s[at, :] * sigma * (1.0 + gate * (1.0 - sigma))).astype(BF16)
        d_s[UP, at, :] = (dh * (gate * sigma)).astype(BF16)

    loop(0, L // CH, backward)
    for c in d_out[GATE] + d_out[UP]:
        c.start()
    make_own(GATE)
    make_own(UP)
    pass_on(GATE, WHOLE)
    pass_on(UP, WHOLE)

    def input_grad(i):
        at = span(i)
        total = dot_t(d_s[GATE], mfull[GATE, at, :]) + dot_t(d_s[UP], mfull[UP, at, :])
        igv[:, at] = total.astype(BF16)

    loop(0, S, input_grad)
    ig_copy.start()
    x_out.wait_recv()
    xpt[...] = xp[...].T
    for c in range(PIECES[DOWN]):
        hand_over(DOWN, c)
    collect(DOWN, WHOLE)
    for c in range(PIECES[DOWN]):
        fold_piece(DOWN, c)
    out_copies[DOWN].start()
    for c in range(PIECES[GATE]):
        make_help(GATE, c)
    hand_over(GATE, WHOLE)
    for c in range(PIECES[GATE]):
        pass_on(GATE, c)
    for c in range(PIECES[UP]):
        make_help(UP, c)
    hand_over(UP, WHOLE)
    for c in range(PIECES[UP]):
        pass_on(UP, c)
    for p in (GATE, UP):
        collect(p, WHOLE)
        for c in range(PIECES[p] + 1):
            if c < PIECES[p]:
                hand_over(p, c)
            if c > 0:
                fold_piece(p, c - 1)
        out_copies[p].start()

    for k in range(1, R):
        coef_copy(k, rep).wait_send()
    loop(1, S, lambda k: merged_copy(UP, k, me).wait_send())
    for c in [x_out, g_out, dh_out] + d_out[GATE] + d_out[UP] + d_out[DOWN]:
        c.wait_send()
    for k in range(1, HS):
        for t in range(2):
            down_copy(t, k, place).wait_send()
    for p in (GATE, UP, DOWN):
        loop(1, HS, lambda k, p=p: own_copy(p, k, place).wait_send())
        for c in range(PIECES[p]):
            loop(1, HS, lambda k, p=p, c=c: help_copy(p, c, k, place).wait_send())
        for c in [*range(PIECES[p]), WHOLE]:
            for j in range(1, chips):
                chip_copy(p, c, j, rep).wait_send()
            for j in range(chips):
                sibling_copy(p, c, j, rep_from(2 * j)).wait_send()
    ig_copy.wait()
    for c in out_copies:
        c.wait()


def place_kernel(n, *refs):
    sources, targets, held, sems = refs[:n], refs[n:2 * n], refs[2 * n:3 * n], refs[3 * n]
    loads = [pltpu.make_async_copy(a, b, sems.at[0, i]) for i, (a, b) in enumerate(zip(sources, held))]
    stores = [pltpu.make_async_copy(a, b, sems.at[1, i]) for i, (a, b) in enumerate(zip(held, targets))]
    for c in loads:
        c.start()
    for a, b in zip(loads, stores):
        a.wait()
        b.start()
    for c in stores:
        c.wait()


def place(arrays):
    n = len(arrays)
    any_spec = pl.BlockSpec(memory_space=pl.ANY)
    return pl.pallas_call(
        functools.partial(place_kernel, n),
        out_shape=tuple(jax.ShapeDtypeStruct(a.shape, a.dtype) for a in arrays),
        in_specs=[any_spec] * n,
        out_specs=(any_spec,) * n,
        scratch_shapes=[pltpu.VMEM(a.shape, a.dtype) for a in arrays] + [pltpu.SemaphoreType.DMA((2, n))],
        compiler_params=pltpu.CompilerParams(vmem_limit_bytes=58 * 1024 * 1024),
        cost_estimate=pl.CostEstimate(flops=0, bytes_accessed=4 * sum(a.size for a in arrays), transcendentals=0),
    )(*arrays)


def fused(S, R, tokens, cotangent, coefficients, w_gate, w_up, w_down):
    E, rows, H = w_gate.shape
    L, D = tokens.shape[1:]
    EL = E // R
    chips = R // 2
    lanes = -(-E // 128) * 128
    any_spec = pl.BlockSpec(memory_space=pl.ANY)
    dma = pltpu.SemaphoreType.DMA
    vmem = pltpu.VMEM
    grad = jax.ShapeDtypeStruct((EL, rows, H), BF16)
    flops = 16 * L * D * H + 2 * 3 * T * rows * H * E * S + 2 * 3 * T * rows * H * EL * R * S
    Q = MOST
    made = pl.pallas_call(
        functools.partial(kernel, S, R),
        out_shape=(jax.ShapeDtypeStruct((1, L, D), BF16), grad, grad, grad),
        in_specs=[pl.BlockSpec(memory_space=vmem)] + [any_spec] * 5,
        out_specs=(any_spec,) * 4,
        scratch_shapes=[
            vmem((L, D), BF16), vmem((L, D), BF16), vmem((D // 2, L), BF16), vmem((D // 2, L), BF16),
            vmem((L, D // 2), BF16), vmem((L, D // 2), BF16), vmem((D // 2, L), BF16), vmem((D // 2, L), BF16),
            vmem((3, E, rows, H), BF16),
            vmem((3, S, rows, H), BF16),
            vmem((2, D, H), BF16),
            vmem((2, D // 2, H), BF16),
            vmem((3, S // 2, rows, H), BF16), vmem((3, S // 2, rows, H), BF16),
            vmem((3, R, S, rows, H), BF16),
            vmem((3, EL, rows, H), BF16),
            vmem((L, D), BF16),
            vmem((R, S, lanes), F32),
            vmem((S * T, E * T), BF16),
            vmem((EL * T, R * S * T), BF16),
            vmem((L, H), F32), vmem((L, H), F32), vmem((L, H), F32),
            vmem((L, H), BF16), vmem((L, H), BF16),
            vmem((3, L, H), BF16), vmem((3, L, H), BF16),
            dma((4 + rows // HEAD,)), dma((4,)),
            dma((2, S)), dma((2, S)), dma((2, S // 2)), dma((2, S // 2)),
            dma((3 + 3 * Q,)), dma((3 + 3 * Q,)),
            dma((3, S // 2)), dma((3, S // 2)), dma((3, Q, S // 2)), dma((3, Q, S // 2)),
            dma((3, Q + 1, chips)), dma((3, Q + 1, chips)), dma((3, Q + 1, chips)), dma((3, Q + 1, chips)),
            dma((R,)), dma((R,)),
        ],
        compiler_params=pltpu.CompilerParams(
            collective_id=0, has_side_effects=True, vmem_limit_bytes=58 * 1024 * 1024),
        cost_estimate=pl.CostEstimate(
            flops=flops, bytes_accessed=2 * (3 * E * rows * H + 3 * L * D + 3 * EL * rows * H),
            transcendentals=2 * L * H),
    )(coefficients, tokens, cotangent, w_gate, w_up, w_down)
    return place(made)


def local(tokens, cotangent, coefficients, w_gate, w_up, w_down):
    mixing = coefficients[0]
    stacked = jnp.stack([w_gate, w_up, w_down])
    merged = jnp.einsum(
        "se,kedh->ksdh", mixing, stacked, preferred_element_type=jnp.float32
    ).astype(jnp.bfloat16)
    arrived = lax.all_to_all(merged, "seg", split_axis=1, concat_axis=2, tiled=True)
    merged_gate = arrived[0, 0]
    merged_up = arrived[1, 0]
    merged_down = arrived[2, 0]
    segment_x = tokens[0]
    segment_g = cotangent[0]
    contract = (((0,), (0,)), ((), ()))
    transposed = (((1,), (1,)), ((), ()))

    def fold_experts(pieces):
        return jnp.einsum("se,ksdh->kedh", mixing, pieces, preferred_element_type=jnp.float32)

    gate_proj = jnp.dot(segment_x, merged_gate, preferred_element_type=jnp.float32)
    up_proj = jnp.dot(segment_x, merged_up, preferred_element_type=jnp.float32)
    sigma = jax.nn.sigmoid(gate_proj)
    activated = gate_proj * sigma
    hidden = (activated * up_proj).astype(jnp.bfloat16)
    grad_down_seg = lax.dot_general(
        segment_g, hidden, contract, preferred_element_type=jnp.float32
    ).astype(jnp.bfloat16)
    down_folded = fold_experts(
        lax.all_to_all(grad_down_seg[None, None], "seg", split_axis=2, concat_axis=1, tiled=True)
    )
    down_summed = lax.psum_scatter(down_folded, "rep", scatter_dimension=1, tiled=True)
    d_hidden = jnp.dot(segment_g, merged_down, preferred_element_type=jnp.float32)
    d_gate = (d_hidden * up_proj * sigma * (1.0 + gate_proj * (1.0 - sigma))).astype(jnp.bfloat16)
    d_up = (d_hidden * activated).astype(jnp.bfloat16)
    input_grad = lax.dot_general(
        d_gate, merged_gate, transposed, preferred_element_type=jnp.float32
    )
    input_grad = input_grad + lax.dot_general(
        d_up, merged_up, transposed, preferred_element_type=jnp.float32
    )
    input_grad = input_grad.astype(jnp.bfloat16)
    grad_gate_seg = lax.dot_general(
        segment_x, d_gate, contract, preferred_element_type=jnp.float32
    ).astype(jnp.bfloat16)
    grad_up_seg = lax.dot_general(
        segment_x, d_up, contract, preferred_element_type=jnp.float32
    ).astype(jnp.bfloat16)
    pair = jnp.stack([grad_gate_seg, grad_up_seg])[:, None]
    pair_folded = fold_experts(lax.all_to_all(pair, "seg", split_axis=2, concat_axis=1, tiled=True))
    pair_summed = lax.psum_scatter(pair_folded, "rep", scatter_dimension=1, tiled=True)
    summed = jnp.concatenate([pair_summed, down_summed], axis=0)
    grads = summed.astype(jnp.bfloat16)
    return (input_grad[None], grads[0], grads[1], grads[2])


def solution(mesh):
    placed = (
        P("rep", "seg", None),
        P("rep", "seg", None),
        P("rep", None, None),
        P(None, "seg", None),
        P(None, "seg", None),
        P(None, "seg", None),
    )
    S, R = mesh.shape["seg"], mesh.shape["rep"]

    def body(tokens, cotangent, coefficients, w_gate, w_up, w_down):
        args = (tokens, cotangent, coefficients, w_gate, w_up, w_down)
        if w_gate.shape[1] % 128 == 0 and w_gate.shape[2] % (128 * MOST) == 0 and R % 2 == 0 and S % 2 == 0 and tokens.shape[1] % 128 == 0:
            return fused(S, R, *args)
        return local(*args)

    return jax.shard_map(
        body,
        mesh=mesh,
        in_specs=placed,
        out_specs=(
            P("rep", "seg", None),
            P("rep", "seg", None),
            P("rep", "seg", None),
            P("rep", "seg", None),
        ),
        check_vma=False,
    )
```

```python
import functools

import jax
import jax.numpy as jnp
from jax import lax
from jax.experimental import pallas as pl
from jax.experimental.pallas import tpu as pltpu
from jax.sharding import PartitionSpec as P

MESH = pl.DeviceIdType.MESH
F32 = jnp.float32
BF16 = jnp.bfloat16
T = 16
GATE, UP, DOWN = 0, 1, 2
Q = 4
HEAD = 32


def one_hot(shape, rows_of, columns_of):
    row = lax.broadcasted_iota(jnp.int32, shape, 0)
    column = lax.broadcasted_iota(jnp.int32, shape, 1)
    return rows_of(row) == columns_of(column)


def dot(a, b):
    return jnp.dot(a, b, preferred_element_type=F32)


def dot_t(a, b):
    return lax.dot_general(a, b, (((1,), (1,)), ((), ())), preferred_element_type=F32)


def kernel(
    S, R, coef_ref, tok_hbm, cot_hbm, wg_hbm, wu_hbm, wd_hbm,
    ig_hbm, gg_hbm, gu_hbm, gd_hbm,
    x, g, xt, gt, xp, gp, xpt, gpt, w, msend, mfull, mdown, gown, ghelp, gall, outv, igv, cbuf, mix, fold,
    gate_s, up_s, dh_s, dhp_s, dhr, d_s, dr,
    load_sem, out_sem, fsend, frecv, dsend, drecv, psend, precv,
    osend, orecv, hsend, hrecv, xsend, xrecv, ssend, srecv, csend, crecv,
):
    me = lax.axis_index("seg")
    rep = lax.axis_index("rep")
    E, rows, H = w.shape[1:]
    EL = outv.shape[1]
    L = x.shape[0]
    chips = R // 2
    sibling = rep + 1 - 2 * lax.rem(rep, 2)
    HS = S // 2
    place = lax.rem(me, HS)
    base = me - place
    other = HS - base
    partner = other + place

    def seg_at(k):
        return lax.rem(me + k, S)

    def seg_from(k):
        return lax.rem(me - k + S, S)

    def place_at(k):
        return lax.rem(place + k, HS)

    def place_from(k):
        return lax.rem(place - k + HS, HS)

    def rep_at(k):
        return lax.rem(rep + k, R)

    def rep_from(k):
        return lax.rem(rep - k + R, R)

    def loop(lo, hi, body):
        lax.fori_loop(lo, hi, lambda i, c: (body(i), c)[1], 0)

    def span(start, count=1):
        return pl.ds(pl.multiple_of(start * rows, rows), count * rows)

    loads = [pltpu.make_async_copy(tok_hbm.at[0], x, load_sem.at[0]),
             pltpu.make_async_copy(cot_hbm.at[0], g, load_sem.at[1])]
    w_loads = {p: pltpu.make_async_copy(h, w.at[p], load_sem.at[1 + p])
               for p, h in ((UP, wu_hbm), (DOWN, wd_hbm))}

    def head(n):
        return pl.ds(n * HEAD, HEAD)

    heads = [pltpu.make_async_copy(wg_hbm.at[:, head(n), :], w.at[GATE, :, head(n), :], load_sem.at[4 + n])
             for n in range(rows // HEAD)]
    for c in heads:
        c.start()

    barrier = pltpu.get_barrier_semaphore()
    for k in range(1, S):
        pl.semaphore_signal(barrier, inc=1, device_id={"seg": seg_at(k)}, device_id_type=MESH)
    for k in range(1, R):
        pl.semaphore_signal(barrier, inc=1, device_id={"rep": rep_at(k)}, device_id_type=MESH)

    coef = coef_ref[0].astype(F32)
    LANES = cbuf.shape[2]
    cbuf[rep] = dot(coef, one_hot((E, LANES), lambda i: i, lambda j: j).astype(F32))
    tall = dot(one_hot((S * T, S), lambda i: i // T, lambda j: j).astype(F32), coef)
    wide = dot(tall, one_hot((E, E * T), lambda i: i, lambda j: j // T).astype(F32))
    keep = one_hot((S * T, E * T), lambda i: i % T, lambda j: j % T)
    mix[...] = jnp.where(keep, wide, 0.0).astype(BF16)

    pl.semaphore_wait(barrier, S - 1 + R - 1)

    def coef_copy(k, owner):
        return pltpu.make_async_remote_copy(
            src_ref=cbuf.at[owner], dst_ref=cbuf.at[owner],
            send_sem=csend.at[k], recv_sem=crecv.at[k],
            device_id={"rep": rep_at(k)}, device_id_type=MESH)

    for k in range(1, R):
        coef_copy(k, rep).start()

    def merged_copy(p, k, owner):
        return pltpu.make_async_remote_copy(
            src_ref=msend.at[p, seg_at(k)], dst_ref=mfull.at[p, span(owner)],
            send_sem=fsend.at[p, k], recv_sem=frecv.at[p, k],
            device_id={"seg": seg_at(k)}, device_id_type=MESH)

    def down_copy(t, k, owner):
        to = place_at(k)
        return pltpu.make_async_remote_copy(
            src_ref=msend.at[DOWN, (base if t == 0 else other) + to], dst_ref=mdown.at[t, span(owner)],
            send_sem=dsend.at[t, k], recv_sem=drecv.at[t, k],
            device_id={"seg": base + to}, device_id_type=MESH)

    def to_partner(n, source, target):
        return pltpu.make_async_remote_copy(
            src_ref=source, dst_ref=target, send_sem=psend.at[n], recv_sem=precv.at[n],
            device_id={"seg": partner}, device_id_type=MESH)

    x_out = to_partner(0, x.at[:, span(other, HS)], xp)
    g_out = to_partner(1, g.at[:, span(other, HS)], gp)
    dh_out = to_partner(2, dhp_s, dhr)
    d_out = [to_partner(3 + p, d_s.at[p], dr.at[p]) for p in (GATE, UP, DOWN)]

    def merge(p, b):
        at = pl.ds(pl.multiple_of(b * T, T), T)
        block = dot(mix[...], w[p, :, at, :].reshape(E * T, H))
        msend[p, :, at, :] = block.astype(BF16).reshape(S, T, H)

    for n, c in enumerate(heads):
        c.wait()
        loop(n * HEAD // T, (n + 1) * HEAD // T, lambda b: merge(GATE, b))

        def send_head(k, n=n):
            pltpu.make_async_remote_copy(
                src_ref=msend.at[GATE, seg_at(k), head(n)],
                dst_ref=mfull.at[GATE, pl.ds(pl.multiple_of(me * rows, rows) + n * HEAD, HEAD)],
                send_sem=fsend.at[GATE, k], recv_sem=frecv.at[GATE, k],
                device_id={"seg": seg_at(k)}, device_id_type=MESH).start()

        loop(1, S, send_head)
        if n == 0:
            for c in list(w_loads.values()) + loads:
                c.start()
    mfull[GATE, span(me), :] = msend[GATE, me]
    w_loads[UP].wait()
    loop(0, rows // T, lambda b: merge(UP, b))
    mfull[UP, span(me), :] = msend[UP, me]
    w_loads[DOWN].wait()
    loop(0, rows // T, lambda b: merge(DOWN, b))
    for k in range(1, HS):
        for t in range(2):
            down_copy(t, k, place).start()
    mdown[0, span(place), :] = msend[DOWN, me]
    mdown[1, span(place), :] = msend[DOWN, partner]

    for c in loads:
        c.wait()
    xt[...] = x[:, span(base, HS)].T
    gt[...] = g[:, span(base, HS)].T
    for k in range(1, R):
        coef_copy(k, rep_from(k)).wait_recv()
    every = cbuf[...].reshape(R * S, LANES)
    mine = one_hot((EL * T, LANES), lambda i: i // T + rep * EL, lambda j: j).astype(F32)
    tall = dot_t(mine, every)
    wide = dot(tall, one_hot((R * S, R * S * T), lambda i: i, lambda j: j // T).astype(F32))
    keep = one_hot((EL * T, R * S * T), lambda i: i % T, lambda j: j % T)
    fold[...] = jnp.where(keep, wide, 0.0).astype(BF16)

    WHOLE = Q
    part = rows // Q

    def piece(c):
        return pl.ds(c * part, part)

    def own_copy(p, k, owner):
        return pltpu.make_async_remote_copy(
            src_ref=gown.at[p, k], dst_ref=gall.at[p, rep, base + owner],
            send_sem=osend.at[p, k], recv_sem=orecv.at[p, k],
            device_id={"seg": base + place_at(k)}, device_id_type=MESH)

    def help_copy(p, c, k, owner):
        return pltpu.make_async_remote_copy(
            src_ref=ghelp.at[p, k, piece(c)], dst_ref=gall.at[p, rep, other + owner, piece(c)],
            send_sem=hsend.at[p, c, k], recv_sem=hrecv.at[p, c, k],
            device_id={"seg": base + place_at(k)}, device_id_type=MESH)

    def unit(p, c, owner):
        if c == WHOLE:
            return gall.at[p, owner, pl.ds(base, HS)]
        return gall.at[p, owner, pl.ds(other, HS), piece(c)]

    def chip_copy(p, c, j, owner):
        block = unit(p, c, owner)
        return pltpu.make_async_remote_copy(
            src_ref=block, dst_ref=block,
            send_sem=xsend.at[p, c, j], recv_sem=xrecv.at[p, c, j],
            device_id={"rep": rep_at(2 * j)}, device_id_type=MESH)

    def sibling_copy(p, c, j, owner):
        block = unit(p, c, owner)
        return pltpu.make_async_remote_copy(
            src_ref=block, dst_ref=block,
            send_sem=ssend.at[p, c, j], recv_sem=srecv.at[p, c, j],
            device_id={"rep": sibling}, device_id_type=MESH)

    def make_own(p):
        transposed = gt if p == DOWN else xt

        def one(k):
            return dot(transposed[span(place_at(k)), :], d_s[p]).astype(BF16)

        def step(k):
            gown[p, k] = one(k)
            own_copy(p, k, place).start()

        loop(1, HS, step)
        gall[p, rep, me] = one(0)

    def make_help(p):
        d_out[p].wait_recv()
        transposed = gpt if p == DOWN else xpt

        def one(k):
            return dot(transposed[span(place_at(k)), :], dr[p]).astype(BF16)

        def step(k):
            ghelp[p, k] = one(k)
            help_copy(p, 0, k, place).start()

        loop(1, HS, step)
        for c in range(1, Q):
            loop(1, HS, lambda k, c=c: help_copy(p, c, k, place).start())
        gall[p, rep, partner] = one(0)

    def pass_on(p, c):
        def arrived(k):
            if c == WHOLE:
                own_copy(p, k, place_from(k)).wait_recv()
            else:
                help_copy(p, c, k, place_from(k)).wait_recv()

        loop(1, HS, arrived)
        for j in range(1, chips):
            chip_copy(p, c, j, rep).start()
        sibling_copy(p, c, 0, rep).start()

    def hand_over(p, c):
        for j in range(1, chips):
            chip_copy(p, c, j, rep_from(2 * j)).wait_recv()
            sibling_copy(p, c, j, rep_from(2 * j)).start()

    def collect(p, c):
        for j in range(chips):
            sibling_copy(p, c, j, lax.rem(sibling - 2 * j + R, R)).wait_recv()

    def fold_piece(p, c):
        collect(p, c)

        def folded(b):
            at = pl.ds(pl.multiple_of(c * part + b * T, T), T)
            block = dot(fold[...], gall[p, :, :, at, :].reshape(R * S * T, H))
            outv[p, :, at, :] = block.astype(BF16).reshape(EL, T, H)

        loop(0, part // T, folded)

    outs = (gg_hbm, gu_hbm, gd_hbm)
    out_copies = [pltpu.make_async_copy(outv.at[p], outs[p], out_sem.at[p]) for p in (GATE, UP, DOWN)]
    ig_copy = pltpu.make_async_copy(igv, ig_hbm.at[0], out_sem.at[3])

    def send_up(k):
        merged_copy(GATE, k, me).wait_send()
        merged_copy(UP, k, me).start()

    loop(1, S, send_up)
    loop(1, S, lambda k: merged_copy(GATE, k, seg_from(k)).wait_recv())
    gate_s[...] = dot(x[...], mfull[GATE])
    for k in range(1, HS):
        for t in range(2):
            down_copy(t, k, place_from(k)).wait_recv()
    dh_s[...] = dot(g[:, span(base, HS)], mdown[0])
    loop(1, S, lambda k: merged_copy(UP, k, me).wait_send())
    g_out.start()
    loop(1, S, lambda k: merged_copy(UP, k, seg_from(k)).wait_recv())
    up_s[...] = dot(x[...], mfull[UP])
    CH = 32

    def chunk(i):
        return pl.ds(pl.multiple_of(i * CH, CH), CH)

    def hidden(i):
        at = chunk(i)
        gate = gate_s[at, :]
        d_s[DOWN, at, :] = (gate * jax.nn.sigmoid(gate) * up_s[at, :]).astype(BF16)

    loop(0, L // CH, hidden)
    d_out[DOWN].start()
    make_own(DOWN)
    g_out.wait_recv()
    dhp_s[...] = dot(gp[...], mdown[1]).astype(BF16)
    dh_out.start()
    gpt[...] = gp[...].T
    pass_on(DOWN, WHOLE)
    make_help(DOWN)
    x_out.start()
    dh_out.wait_recv()

    def backward(i):
        at = chunk(i)
        gate = gate_s[at, :]
        dh = dh_s[at, :] + dhr[at, :].astype(F32)
        sigma = jax.nn.sigmoid(gate)
        d_s[GATE, at, :] = (dh * up_s[at, :] * sigma * (1.0 + gate * (1.0 - sigma))).astype(BF16)
        d_s[UP, at, :] = (dh * (gate * sigma)).astype(BF16)

    loop(0, L // CH, backward)
    d_out[GATE].start()
    make_own(GATE)
    make_own(UP)
    for c in range(Q):
        pass_on(DOWN, c)
    pass_on(GATE, WHOLE)
    pass_on(UP, WHOLE)
    hand_over(DOWN, WHOLE)

    def input_grad(i):
        at = span(i)
        total = dot_t(d_s[GATE], mfull[GATE, at, :]) + dot_t(d_s[UP], mfull[UP, at, :])
        igv[:, at] = total.astype(BF16)

    loop(0, S, input_grad)
    ig_copy.start()
    x_out.wait_recv()
    xpt[...] = xp[...].T
    d_out[GATE].wait_send()
    d_out[UP].start()
    for c in range(Q):
        hand_over(DOWN, c)
    collect(DOWN, WHOLE)
    make_help(GATE)
    for c in range(Q):
        fold_piece(DOWN, c)
    out_copies[DOWN].start()
    hand_over(GATE, WHOLE)
    for c in range(Q):
        pass_on(GATE, c)
    make_help(UP)
    hand_over(UP, WHOLE)
    for c in range(Q):
        pass_on(UP, c)
    for p in (GATE, UP):
        collect(p, WHOLE)
        for c in range(Q + 1):
            if c < Q:
                hand_over(p, c)
            if c > 0:
                fold_piece(p, c - 1)
        out_copies[p].start()

    for k in range(1, R):
        coef_copy(k, rep).wait_send()
    for c in (x_out, g_out, dh_out, d_out[UP], d_out[DOWN]):
        c.wait_send()
    for k in range(1, HS):
        for t in range(2):
            down_copy(t, k, place).wait_send()
    for p in (GATE, UP, DOWN):
        loop(1, HS, lambda k, p=p: own_copy(p, k, place).wait_send())
        for c in range(Q):
            loop(1, HS, lambda k, p=p, c=c: help_copy(p, c, k, place).wait_send())
        for c in [*range(Q), WHOLE]:
            for j in range(1, chips):
                chip_copy(p, c, j, rep).wait_send()
            for j in range(chips):
                sibling_copy(p, c, j, rep_from(2 * j)).wait_send()
    ig_copy.wait()
    for c in out_copies:
        c.wait()


def place_kernel(n, *refs):
    sources, targets, held, sems = refs[:n], refs[n:2 * n], refs[2 * n:3 * n], refs[3 * n]
    loads = [pltpu.make_async_copy(a, b, sems.at[0, i]) for i, (a, b) in enumerate(zip(sources, held))]
    stores = [pltpu.make_async_copy(a, b, sems.at[1, i]) for i, (a, b) in enumerate(zip(held, targets))]
    for c in loads:
        c.start()
    for a, b in zip(loads, stores):
        a.wait()
        b.start()
    for c in stores:
        c.wait()


def place(arrays):
    n = len(arrays)
    any_spec = pl.BlockSpec(memory_space=pl.ANY)
    return pl.pallas_call(
        functools.partial(place_kernel, n),
        out_shape=tuple(jax.ShapeDtypeStruct(a.shape, a.dtype) for a in arrays),
        in_specs=[any_spec] * n,
        out_specs=(any_spec,) * n,
        scratch_shapes=[pltpu.VMEM(a.shape, a.dtype) for a in arrays] + [pltpu.SemaphoreType.DMA((2, n))],
        compiler_params=pltpu.CompilerParams(vmem_limit_bytes=58 * 1024 * 1024),
        cost_estimate=pl.CostEstimate(flops=0, bytes_accessed=4 * sum(a.size for a in arrays), transcendentals=0),
    )(*arrays)


def fused(S, R, tokens, cotangent, coefficients, w_gate, w_up, w_down):
    E, rows, H = w_gate.shape
    L, D = tokens.shape[1:]
    EL = E // R
    chips = R // 2
    lanes = -(-E // 128) * 128
    any_spec = pl.BlockSpec(memory_space=pl.ANY)
    dma = pltpu.SemaphoreType.DMA
    vmem = pltpu.VMEM
    grad = jax.ShapeDtypeStruct((EL, rows, H), BF16)
    flops = 16 * L * D * H + 2 * 3 * T * rows * H * E * S + 2 * 3 * T * rows * H * EL * R * S
    made = pl.pallas_call(
        functools.partial(kernel, S, R),
        out_shape=(jax.ShapeDtypeStruct((1, L, D), BF16), grad, grad, grad),
        in_specs=[pl.BlockSpec(memory_space=vmem)] + [any_spec] * 5,
        out_specs=(any_spec,) * 4,
        scratch_shapes=[
            vmem((L, D), BF16), vmem((L, D), BF16), vmem((D // 2, L), BF16), vmem((D // 2, L), BF16),
            vmem((L, D // 2), BF16), vmem((L, D // 2), BF16), vmem((D // 2, L), BF16), vmem((D // 2, L), BF16),
            vmem((3, E, rows, H), BF16),
            vmem((3, S, rows, H), BF16),
            vmem((2, D, H), BF16),
            vmem((2, D // 2, H), BF16),
            vmem((3, S // 2, rows, H), BF16), vmem((3, S // 2, rows, H), BF16),
            vmem((3, R, S, rows, H), BF16),
            vmem((3, EL, rows, H), BF16),
            vmem((L, D), BF16),
            vmem((R, S, lanes), F32),
            vmem((S * T, E * T), BF16),
            vmem((EL * T, R * S * T), BF16),
            vmem((L, H), F32), vmem((L, H), F32), vmem((L, H), F32),
            vmem((L, H), BF16), vmem((L, H), BF16),
            vmem((3, L, H), BF16), vmem((3, L, H), BF16),
            dma((4 + rows // HEAD,)), dma((4,)),
            dma((2, S)), dma((2, S)), dma((2, S // 2)), dma((2, S // 2)),
            dma((6,)), dma((6,)),
            dma((3, S // 2)), dma((3, S // 2)), dma((3, Q, S // 2)), dma((3, Q, S // 2)),
            dma((3, Q + 1, chips)), dma((3, Q + 1, chips)), dma((3, Q + 1, chips)), dma((3, Q + 1, chips)),
            dma((R,)), dma((R,)),
        ],
        compiler_params=pltpu.CompilerParams(
            collective_id=0, has_side_effects=True, vmem_limit_bytes=58 * 1024 * 1024),
        cost_estimate=pl.CostEstimate(
            flops=flops, bytes_accessed=2 * (3 * E * rows * H + 3 * L * D + 3 * EL * rows * H),
            transcendentals=2 * L * H),
    )(coefficients, tokens, cotangent, w_gate, w_up, w_down)
    return place(made)


def local(tokens, cotangent, coefficients, w_gate, w_up, w_down):
    mixing = coefficients[0]
    stacked = jnp.stack([w_gate, w_up, w_down])
    merged = jnp.einsum(
        "se,kedh->ksdh", mixing, stacked, preferred_element_type=jnp.float32
    ).astype(jnp.bfloat16)
    arrived = lax.all_to_all(merged, "seg", split_axis=1, concat_axis=2, tiled=True)
    merged_gate = arrived[0, 0]
    merged_up = arrived[1, 0]
    merged_down = arrived[2, 0]
    segment_x = tokens[0]
    segment_g = cotangent[0]
    contract = (((0,), (0,)), ((), ()))
    transposed = (((1,), (1,)), ((), ()))

    def fold_experts(pieces):
        return jnp.einsum("se,ksdh->kedh", mixing, pieces, preferred_element_type=jnp.float32)

    gate_proj = jnp.dot(segment_x, merged_gate, preferred_element_type=jnp.float32)
    up_proj = jnp.dot(segment_x, merged_up, preferred_element_type=jnp.float32)
    sigma = jax.nn.sigmoid(gate_proj)
    activated = gate_proj * sigma
    hidden = (activated * up_proj).astype(jnp.bfloat16)
    grad_down_seg = lax.dot_general(
        segment_g, hidden, contract, preferred_element_type=jnp.float32
    ).astype(jnp.bfloat16)
    down_folded = fold_experts(
        lax.all_to_all(grad_down_seg[None, None], "seg", split_axis=2, concat_axis=1, tiled=True)
    )
    down_summed = lax.psum_scatter(down_folded, "rep", scatter_dimension=1, tiled=True)
    d_hidden = jnp.dot(segment_g, merged_down, preferred_element_type=jnp.float32)
    d_gate = (d_hidden * up_proj * sigma * (1.0 + gate_proj * (1.0 - sigma))).astype(jnp.bfloat16)
    d_up = (d_hidden * activated).astype(jnp.bfloat16)
    input_grad = lax.dot_general(
        d_gate, merged_gate, transposed, preferred_element_type=jnp.float32
    )
    input_grad = input_grad + lax.dot_general(
        d_up, merged_up, transposed, preferred_element_type=jnp.float32
    )
    input_grad = input_grad.astype(jnp.bfloat16)
    grad_gate_seg = lax.dot_general(
        segment_x, d_gate, contract, preferred_element_type=jnp.float32
    ).astype(jnp.bfloat16)
    grad_up_seg = lax.dot_general(
        segment_x, d_up, contract, preferred_element_type=jnp.float32
    ).astype(jnp.bfloat16)
    pair = jnp.stack([grad_gate_seg, grad_up_seg])[:, None]
    pair_folded = fold_experts(lax.all_to_all(pair, "seg", split_axis=2, concat_axis=1, tiled=True))
    pair_summed = lax.psum_scatter(pair_folded, "rep", scatter_dimension=1, tiled=True)
    summed = jnp.concatenate([pair_summed, down_summed], axis=0)
    grads = summed.astype(jnp.bfloat16)
    return (input_grad[None], grads[0], grads[1], grads[2])


def solution(mesh):
    placed = (
        P("rep", "seg", None),
        P("rep", "seg", None),
        P("rep", None, None),
        P(None, "seg", None),
        P(None, "seg", None),
        P(None, "seg", None),
    )
    S, R = mesh.shape["seg"], mesh.shape["rep"]

    def body(tokens, cotangent, coefficients, w_gate, w_up, w_down):
        args = (tokens, cotangent, coefficients, w_gate, w_up, w_down)
        if w_gate.shape[1] % 128 == 0 and R % 2 == 0 and S % 2 == 0 and tokens.shape[1] % 128 == 0:
            return fused(S, R, *args)
        return local(*args)

    return jax.shard_map(
        body,
        mesh=mesh,
        in_specs=placed,
        out_specs=(
            P("rep", "seg", None),
            P("rep", "seg", None),
            P("rep", "seg", None),
            P("rep", "seg", None),
        ),
        check_vma=False,
    )
```

```python
import functools

import jax
import jax.numpy as jnp
from jax import lax
from jax.experimental import pallas as pl
from jax.experimental.pallas import tpu as pltpu
from jax.sharding import PartitionSpec as P

MESH = pl.DeviceIdType.MESH
F32 = jnp.float32
BF16 = jnp.bfloat16
T = 16
GATE, UP, DOWN = 0, 2, 4
Q = 2
HEAD = 32


def one_hot(shape, rows_of, columns_of):
    row = lax.broadcasted_iota(jnp.int32, shape, 0)
    column = lax.broadcasted_iota(jnp.int32, shape, 1)
    return rows_of(row) == columns_of(column)


def dot(a, b):
    return jnp.dot(a, b, preferred_element_type=F32)


def dot_t(a, b):
    return lax.dot_general(a, b, (((1,), (1,)), ((), ())), preferred_element_type=F32)


def kernel(
    S, R, coef_ref, tok_hbm, cot_hbm, wg_hbm, wu_hbm, wd_hbm,
    ig_hbm, gg_hbm, gu_hbm, gd_hbm,
    x, g, xt, gt, xp, gp, xpt, gpt, w, msend, mfull, mdown, gown, ghelp, gall, outv, igv, cbuf, mix, fold,
    gate_s, up_s, dh_s, dhp_s, dhr, d_s, dr,
    load_sem, out_sem, fsend, frecv, dsend, drecv, psend, precv,
    osend, orecv, hsend, hrecv, xsend, xrecv, ssend, srecv, csend, crecv,
):
    me = lax.axis_index("seg")
    rep = lax.axis_index("rep")
    E, rows, H = w.shape[1:]
    HH = H // 2
    EL = outv.shape[1]
    L = x.shape[0]
    chips = R // 2
    sibling = rep + 1 - 2 * lax.rem(rep, 2)
    HS = S // 2
    place = lax.rem(me, HS)
    base = me - place
    other = HS - base
    partner = other + place

    def seg_at(k):
        return lax.rem(me + k, S)

    def seg_from(k):
        return lax.rem(me - k + S, S)

    def place_at(k):
        return lax.rem(place + k, HS)

    def place_from(k):
        return lax.rem(place - k + HS, HS)

    def rep_at(k):
        return lax.rem(rep + k, R)

    def rep_from(k):
        return lax.rem(rep - k + R, R)

    def loop(lo, hi, body):
        lax.fori_loop(lo, hi, lambda i, c: (body(i), c)[1], 0)

    def span(start, count=1):
        return pl.ds(pl.multiple_of(start * rows, rows), count * rows)

    loads = [pltpu.make_async_copy(tok_hbm.at[0], x, load_sem.at[0]),
             pltpu.make_async_copy(cot_hbm.at[0], g, load_sem.at[1])]
    w_loads = {p: pltpu.make_async_copy(h, w.at[p // 2], load_sem.at[1 + p // 2])
               for p, h in ((UP, wu_hbm), (DOWN, wd_hbm))}

    def head(n):
        return pl.ds(n * HEAD, HEAD)

    heads = [pltpu.make_async_copy(wg_hbm.at[:, head(n), :], w.at[GATE, :, head(n), :], load_sem.at[4 + n])
             for n in range(rows // HEAD)]
    for c in heads:
        c.start()

    barrier = pltpu.get_barrier_semaphore()
    for k in range(1, S):
        pl.semaphore_signal(barrier, inc=1, device_id={"seg": seg_at(k)}, device_id_type=MESH)
    for k in range(1, R):
        pl.semaphore_signal(barrier, inc=1, device_id={"rep": rep_at(k)}, device_id_type=MESH)

    coef = coef_ref[0].astype(F32)
    LANES = cbuf.shape[2]
    cbuf[rep] = dot(coef, one_hot((E, LANES), lambda i: i, lambda j: j).astype(F32))
    tall = dot(one_hot((S * T, S), lambda i: i // T, lambda j: j).astype(F32), coef)
    wide = dot(tall, one_hot((E, E * T), lambda i: i, lambda j: j // T).astype(F32))
    keep = one_hot((S * T, E * T), lambda i: i % T, lambda j: j % T)
    mix[...] = jnp.where(keep, wide, 0.0).astype(BF16)

    pl.semaphore_wait(barrier, S - 1 + R - 1)

    def coef_copy(k, owner):
        return pltpu.make_async_remote_copy(
            src_ref=cbuf.at[owner], dst_ref=cbuf.at[owner],
            send_sem=csend.at[k], recv_sem=crecv.at[k],
            device_id={"rep": rep_at(k)}, device_id_type=MESH)

    for k in range(1, R):
        coef_copy(k, rep).start()

    def merged_copy(p, k, owner):
        return pltpu.make_async_remote_copy(
            src_ref=msend.at[p, seg_at(k)], dst_ref=mfull.at[p, span(owner)],
            send_sem=fsend.at[p, k], recv_sem=frecv.at[p, k],
            device_id={"seg": seg_at(k)}, device_id_type=MESH)

    def down_copy(h, t, k, owner):
        to = place_at(k)
        return pltpu.make_async_remote_copy(
            src_ref=msend.at[DOWN + h, (base if t == 0 else other) + to], dst_ref=mdown.at[h, t, span(owner)],
            send_sem=dsend.at[h, t, k], recv_sem=drecv.at[h, t, k],
            device_id={"seg": base + to}, device_id_type=MESH)

    def to_partner(n, source, target):
        return pltpu.make_async_remote_copy(
            src_ref=source, dst_ref=target, send_sem=psend.at[n], recv_sem=precv.at[n],
            device_id={"seg": partner}, device_id_type=MESH)

    x_out = to_partner(0, x.at[:, span(other, HS)], xp)
    g_out = to_partner(1, g.at[:, span(other, HS)], gp)
    dh_out = [to_partner(2 + h, dhp_s.at[h], dhr.at[h]) for h in range(2)]
    d_out = [to_partner(4 + p, d_s.at[p], dr.at[p]) for p in range(6)]

    def merge(p, b):
        at = pl.ds(pl.multiple_of(b * T, T), T)
        block = dot(mix[...], w[p // 2, :, at, :].reshape(E * T, H)).astype(BF16)
        for h in range(2):
            msend[p + h, :, at, :] = block[:, h * HH:(h + 1) * HH].reshape(S, T, HH)

    for n, c in enumerate(heads):
        c.wait()
        loop(n * HEAD // T, (n + 1) * HEAD // T, lambda b: merge(GATE, b))

        def send_head(k, n=n):
            pltpu.make_async_remote_copy(
                src_ref=msend.at[GATE, seg_at(k), head(n)],
                dst_ref=mfull.at[GATE, pl.ds(pl.multiple_of(me * rows, rows) + n * HEAD, HEAD)],
                send_sem=fsend.at[GATE, k], recv_sem=frecv.at[GATE, k],
                device_id={"seg": seg_at(k)}, device_id_type=MESH).start()

        loop(1, S, send_head)
        if n == 0:
            for c in list(w_loads.values()) + loads:
                c.start()

    def send_down(h):
        for k in range(1, HS):
            for t in range(2):
                down_copy(h, t, k, place).start()

    w_loads[UP].wait()
    loop(0, rows // T, lambda b: merge(UP, b))
    for v in (GATE, GATE + 1, UP, UP + 1):
        mfull[v, span(me), :] = msend[v, me]
    w_loads[DOWN].wait()
    loop(0, rows // T, lambda b: merge(DOWN, b))
    send_down(0)
    for h in range(2):
        mdown[h, 0, span(place), :] = msend[DOWN + h, me]
        mdown[h, 1, span(place), :] = msend[DOWN + h, partner]

    for c in loads:
        c.wait()
    xt[...] = x[:, span(base, HS)].T
    gt[...] = g[:, span(base, HS)].T
    for k in range(1, R):
        coef_copy(k, rep_from(k)).wait_recv()
    every = cbuf[...].reshape(R * S, LANES)
    mine = one_hot((EL * T, LANES), lambda i: i // T + rep * EL, lambda j: j).astype(F32)
    tall = dot_t(mine, every)
    wide = dot(tall, one_hot((R * S, R * S * T), lambda i: i, lambda j: j // T).astype(F32))
    keep = one_hot((EL * T, R * S * T), lambda i: i % T, lambda j: j % T)
    fold[...] = jnp.where(keep, wide, 0.0).astype(BF16)

    WHOLE = Q
    part = rows // Q

    def piece(c):
        return pl.ds(c * part, part)

    def own_copy(p, k, owner):
        return pltpu.make_async_remote_copy(
            src_ref=gown.at[p, k], dst_ref=gall.at[p, rep, base + owner],
            send_sem=osend.at[p, k], recv_sem=orecv.at[p, k],
            device_id={"seg": base + place_at(k)}, device_id_type=MESH)

    def help_copy(p, c, k, owner):
        return pltpu.make_async_remote_copy(
            src_ref=ghelp.at[p, k, piece(c)], dst_ref=gall.at[p, rep, other + owner, piece(c)],
            send_sem=hsend.at[p, c, k], recv_sem=hrecv.at[p, c, k],
            device_id={"seg": base + place_at(k)}, device_id_type=MESH)

    def unit(p, c, owner):
        if c == WHOLE:
            return gall.at[p, owner, pl.ds(base, HS)]
        return gall.at[p, owner, pl.ds(other, HS), piece(c)]

    def chip_copy(p, c, j, owner):
        block = unit(p, c, owner)
        return pltpu.make_async_remote_copy(
            src_ref=block, dst_ref=block,
            send_sem=xsend.at[p, c, j], recv_sem=xrecv.at[p, c, j],
            device_id={"rep": rep_at(2 * j)}, device_id_type=MESH)

    def sibling_copy(p, c, j, owner):
        block = unit(p, c, owner)
        return pltpu.make_async_remote_copy(
            src_ref=block, dst_ref=block,
            send_sem=ssend.at[p, c, j], recv_sem=srecv.at[p, c, j],
            device_id={"rep": sibling}, device_id_type=MESH)

    def make_own(p):
        transposed = gt if p >= DOWN else xt

        def one(k):
            return dot(transposed[span(place_at(k)), :], d_s[p]).astype(BF16)

        def step(k):
            gown[p, k] = one(k)
            own_copy(p, k, place).start()

        loop(1, HS, step)
        gall[p, rep, me] = one(0)

    def make_help(p):
        d_out[p].wait_recv()
        transposed = gpt if p >= DOWN else xpt

        def one(k):
            return dot(transposed[span(place_at(k)), :], dr[p]).astype(BF16)

        def step(k):
            ghelp[p, k] = one(k)
            help_copy(p, 0, k, place).start()

        loop(1, HS, step)
        for c in range(1, Q):
            loop(1, HS, lambda k, c=c: help_copy(p, c, k, place).start())
        gall[p, rep, partner] = one(0)

    def pass_on(p, c):
        def arrived(k):
            if c == WHOLE:
                own_copy(p, k, place_from(k)).wait_recv()
            else:
                help_copy(p, c, k, place_from(k)).wait_recv()

        loop(1, HS, arrived)
        for j in range(1, chips):
            chip_copy(p, c, j, rep).start()
        sibling_copy(p, c, 0, rep).start()

    def hand_over(p, c):
        for j in range(1, chips):
            chip_copy(p, c, j, rep_from(2 * j)).wait_recv()
            sibling_copy(p, c, j, rep_from(2 * j)).start()

    def collect(p, c):
        for j in range(chips):
            sibling_copy(p, c, j, lax.rem(sibling - 2 * j + R, R)).wait_recv()

    def fold_piece(p, c):
        collect(p, c)

        def folded(b):
            at = pl.ds(pl.multiple_of(c * part + b * T, T), T)
            block = dot(fold[...], gall[p, :, :, at, :].reshape(R * S * T, HH))
            lanes = pl.ds(p % 2 * HH, HH)
            outv[p // 2, :, at, lanes] = block.astype(BF16).reshape(EL, T, HH)

        loop(0, part // T, folded)

    outs = (gg_hbm, gu_hbm, gd_hbm)
    out_copies = [pltpu.make_async_copy(outv.at[n], outs[n], out_sem.at[n]) for n in range(3)]
    ig_copy = pltpu.make_async_copy(igv, ig_hbm.at[0], out_sem.at[3])

    def send_after(p, before):
        def step(k):
            merged_copy(before, k, me).wait_send()
            merged_copy(p, k, me).start()

        loop(1, S, step)

    def arrive(p):
        loop(1, S, lambda k: merged_copy(p, k, seg_from(k)).wait_recv())

    def project_gate(h):
        arrive(GATE + h)
        gate_s[h] = dot(x[...], mfull[GATE + h])

    def project_down(h):
        for k in range(1, HS):
            for t in range(2):
                down_copy(h, t, k, place_from(k)).wait_recv()
        dh_s[h] = dot(g[:, span(base, HS)], mdown[h, 0])

    CH = 32

    def chunk(i):
        return pl.ds(pl.multiple_of(i * CH, CH), CH)

    def make_hidden(h):
        arrive(UP + h)
        up_s[h] = dot(x[...], mfull[UP + h])

        def hidden(i):
            at = chunk(i)
            gate = gate_s[h, at, :]
            d_s[DOWN + h, at, :] = (gate * jax.nn.sigmoid(gate) * up_s[h, at, :]).astype(BF16)

        loop(0, L // CH, hidden)
        d_out[DOWN + h].start()
        make_own(DOWN + h)

    def help_down(h):
        dhp_s[h] = dot(gp[...], mdown[h, 1]).astype(BF16)
        dh_out[h].start()

    def make_d(h):
        dh_out[h].wait_recv()

        def backward(i):
            at = chunk(i)
            gate = gate_s[h, at, :]
            dh = dh_s[h, at, :] + dhr[h, at, :].astype(F32)
            sigma = jax.nn.sigmoid(gate)
            d_s[GATE + h, at, :] = (dh * up_s[h, at, :] * sigma * (1.0 + gate * (1.0 - sigma))).astype(BF16)
            d_s[UP + h, at, :] = (dh * (gate * sigma)).astype(BF16)

        loop(0, L // CH, backward)
        d_out[GATE + h].start()
        d_out[UP + h].start()
        make_own(GATE + h)
        make_own(UP + h)

    def pass_pieces(p):
        for c in range(Q):
            pass_on(p, c)

    def finish(p):
        collect(p, WHOLE)
        for c in range(Q + 1):
            if c < Q:
                hand_over(p, c)
            if c > 0:
                fold_piece(p, c - 1)

    send_after(UP, GATE)
    project_gate(0)
    g_out.start()
    project_down(0)
    send_after(GATE + 1, UP)
    make_hidden(0)
    send_down(1)
    g_out.wait_recv()
    help_down(0)
    gpt[...] = gp[...].T
    pass_on(DOWN, WHOLE)
    x_out.start()
    make_help(DOWN)
    send_after(UP + 1, GATE + 1)
    make_d(0)
    pass_pieces(DOWN)
    pass_on(GATE, WHOLE)
    pass_on(UP, WHOLE)
    project_gate(1)
    project_down(1)
    help_down(1)
    hand_over(DOWN, WHOLE)
    make_hidden(1)
    x_out.wait_recv()
    xpt[...] = xp[...].T
    make_help(GATE)
    make_help(UP)
    pass_on(DOWN + 1, WHOLE)
    pass_pieces(GATE)
    pass_pieces(UP)
    make_help(DOWN + 1)
    make_d(1)
    pass_pieces(DOWN + 1)
    pass_on(GATE + 1, WHOLE)
    pass_on(UP + 1, WHOLE)

    def input_grad(i):
        at = span(i)
        total = sum(dot_t(d_s[v], mfull[v, at, :]) for v in (GATE, GATE + 1, UP, UP + 1))
        igv[:, at] = total.astype(BF16)

    loop(0, S, input_grad)
    ig_copy.start()
    finish(DOWN)
    hand_over(GATE, WHOLE)
    hand_over(UP, WHOLE)
    make_help(GATE + 1)
    make_help(UP + 1)
    pass_pieces(GATE + 1)
    finish(GATE)
    pass_pieces(UP + 1)
    finish(UP)
    hand_over(DOWN + 1, WHOLE)
    hand_over(GATE + 1, WHOLE)
    hand_over(UP + 1, WHOLE)
    for p, n in ((DOWN, 2), (GATE, 0), (UP, 1)):
        finish(p + 1)
        out_copies[n].start()

    for k in range(1, R):
        coef_copy(k, rep).wait_send()
    loop(1, S, lambda k: merged_copy(UP + 1, k, me).wait_send())
    for c in [x_out, g_out] + dh_out + d_out:
        c.wait_send()
    for k in range(1, HS):
        for h in range(2):
            for t in range(2):
                down_copy(h, t, k, place).wait_send()
    for p in range(6):
        loop(1, HS, lambda k, p=p: own_copy(p, k, place).wait_send())
        for c in range(Q):
            loop(1, HS, lambda k, p=p, c=c: help_copy(p, c, k, place).wait_send())
        for c in [*range(Q), WHOLE]:
            for j in range(1, chips):
                chip_copy(p, c, j, rep).wait_send()
            for j in range(chips):
                sibling_copy(p, c, j, rep_from(2 * j)).wait_send()
    ig_copy.wait()
    for c in out_copies:
        c.wait()


def place_kernel(n, *refs):
    sources, targets, held, sems = refs[:n], refs[n:2 * n], refs[2 * n:3 * n], refs[3 * n]
    loads = [pltpu.make_async_copy(a, b, sems.at[0, i]) for i, (a, b) in enumerate(zip(sources, held))]
    stores = [pltpu.make_async_copy(a, b, sems.at[1, i]) for i, (a, b) in enumerate(zip(held, targets))]
    for c in loads:
        c.start()
    for a, b in zip(loads, stores):
        a.wait()
        b.start()
    for c in stores:
        c.wait()


def place(arrays):
    n = len(arrays)
    any_spec = pl.BlockSpec(memory_space=pl.ANY)
    return pl.pallas_call(
        functools.partial(place_kernel, n),
        out_shape=tuple(jax.ShapeDtypeStruct(a.shape, a.dtype) for a in arrays),
        in_specs=[any_spec] * n,
        out_specs=(any_spec,) * n,
        scratch_shapes=[pltpu.VMEM(a.shape, a.dtype) for a in arrays] + [pltpu.SemaphoreType.DMA((2, n))],
        compiler_params=pltpu.CompilerParams(vmem_limit_bytes=58 * 1024 * 1024),
        cost_estimate=pl.CostEstimate(flops=0, bytes_accessed=4 * sum(a.size for a in arrays), transcendentals=0),
    )(*arrays)


def fused(S, R, tokens, cotangent, coefficients, w_gate, w_up, w_down):
    E, rows, H = w_gate.shape
    L, D = tokens.shape[1:]
    EL = E // R
    HH = H // 2
    chips = R // 2
    lanes = -(-E // 128) * 128
    any_spec = pl.BlockSpec(memory_space=pl.ANY)
    dma = pltpu.SemaphoreType.DMA
    vmem = pltpu.VMEM
    grad = jax.ShapeDtypeStruct((EL, rows, H), BF16)
    flops = 16 * L * D * H + 2 * 3 * T * rows * H * E * S + 2 * 3 * T * rows * H * EL * R * S
    made = pl.pallas_call(
        functools.partial(kernel, S, R),
        out_shape=(jax.ShapeDtypeStruct((1, L, D), BF16), grad, grad, grad),
        in_specs=[pl.BlockSpec(memory_space=vmem)] + [any_spec] * 5,
        out_specs=(any_spec,) * 4,
        scratch_shapes=[
            vmem((L, D), BF16), vmem((L, D), BF16), vmem((D // 2, L), BF16), vmem((D // 2, L), BF16),
            vmem((L, D // 2), BF16), vmem((L, D // 2), BF16), vmem((D // 2, L), BF16), vmem((D // 2, L), BF16),
            vmem((3, E, rows, H), BF16),
            vmem((6, S, rows, HH), BF16),
            vmem((4, D, HH), BF16),
            vmem((2, 2, D // 2, HH), BF16),
            vmem((6, S // 2, rows, HH), BF16), vmem((6, S // 2, rows, HH), BF16),
            vmem((6, R, S, rows, HH), BF16),
            vmem((3, EL, rows, H), BF16),
            vmem((L, D), BF16),
            vmem((R, S, lanes), F32),
            vmem((S * T, E * T), BF16),
            vmem((EL * T, R * S * T), BF16),
            vmem((2, L, HH), F32), vmem((2, L, HH), F32), vmem((2, L, HH), F32),
            vmem((2, L, HH), BF16), vmem((2, L, HH), BF16),
            vmem((6, L, HH), BF16), vmem((6, L, HH), BF16),
            dma((4 + rows // HEAD,)), dma((4,)),
            dma((4, S)), dma((4, S)), dma((2, 2, S // 2)), dma((2, 2, S // 2)),
            dma((10,)), dma((10,)),
            dma((6, S // 2)), dma((6, S // 2)), dma((6, Q, S // 2)), dma((6, Q, S // 2)),
            dma((6, Q + 1, chips)), dma((6, Q + 1, chips)), dma((6, Q + 1, chips)), dma((6, Q + 1, chips)),
            dma((R,)), dma((R,)),
        ],
        compiler_params=pltpu.CompilerParams(
            collective_id=0, has_side_effects=True, vmem_limit_bytes=58 * 1024 * 1024),
        cost_estimate=pl.CostEstimate(
            flops=flops, bytes_accessed=2 * (3 * E * rows * H + 3 * L * D + 3 * EL * rows * H),
            transcendentals=2 * L * H),
    )(coefficients, tokens, cotangent, w_gate, w_up, w_down)
    return place(made)


def local(tokens, cotangent, coefficients, w_gate, w_up, w_down):
    mixing = coefficients[0]
    stacked = jnp.stack([w_gate, w_up, w_down])
    merged = jnp.einsum(
        "se,kedh->ksdh", mixing, stacked, preferred_element_type=jnp.float32
    ).astype(jnp.bfloat16)
    arrived = lax.all_to_all(merged, "seg", split_axis=1, concat_axis=2, tiled=True)
    merged_gate = arrived[0, 0]
    merged_up = arrived[1, 0]
    merged_down = arrived[2, 0]
    segment_x = tokens[0]
    segment_g = cotangent[0]
    contract = (((0,), (0,)), ((), ()))
    transposed = (((1,), (1,)), ((), ()))

    def fold_experts(pieces):
        return jnp.einsum("se,ksdh->kedh", mixing, pieces, preferred_element_type=jnp.float32)

    gate_proj = jnp.dot(segment_x, merged_gate, preferred_element_type=jnp.float32)
    up_proj = jnp.dot(segment_x, merged_up, preferred_element_type=jnp.float32)
    sigma = jax.nn.sigmoid(gate_proj)
    activated = gate_proj * sigma
    hidden = (activated * up_proj).astype(jnp.bfloat16)
    grad_down_seg = lax.dot_general(
        segment_g, hidden, contract, preferred_element_type=jnp.float32
    ).astype(jnp.bfloat16)
    down_folded = fold_experts(
        lax.all_to_all(grad_down_seg[None, None], "seg", split_axis=2, concat_axis=1, tiled=True)
    )
    down_summed = lax.psum_scatter(down_folded, "rep", scatter_dimension=1, tiled=True)
    d_hidden = jnp.dot(segment_g, merged_down, preferred_element_type=jnp.float32)
    d_gate = (d_hidden * up_proj * sigma * (1.0 + gate_proj * (1.0 - sigma))).astype(jnp.bfloat16)
    d_up = (d_hidden * activated).astype(jnp.bfloat16)
    input_grad = lax.dot_general(
        d_gate, merged_gate, transposed, preferred_element_type=jnp.float32
    )
    input_grad = input_grad + lax.dot_general(
        d_up, merged_up, transposed, preferred_element_type=jnp.float32
    )
    input_grad = input_grad.astype(jnp.bfloat16)
    grad_gate_seg = lax.dot_general(
        segment_x, d_gate, contract, preferred_element_type=jnp.float32
    ).astype(jnp.bfloat16)
    grad_up_seg = lax.dot_general(
        segment_x, d_up, contract, preferred_element_type=jnp.float32
    ).astype(jnp.bfloat16)
    pair = jnp.stack([grad_gate_seg, grad_up_seg])[:, None]
    pair_folded = fold_experts(lax.all_to_all(pair, "seg", split_axis=2, concat_axis=1, tiled=True))
    pair_summed = lax.psum_scatter(pair_folded, "rep", scatter_dimension=1, tiled=True)
    summed = jnp.concatenate([pair_summed, down_summed], axis=0)
    grads = summed.astype(jnp.bfloat16)
    return (input_grad[None], grads[0], grads[1], grads[2])


def solution(mesh):
    placed = (
        P("rep", "seg", None),
        P("rep", "seg", None),
        P("rep", None, None),
        P(None, "seg", None),
        P(None, "seg", None),
        P(None, "seg", None),
    )
    S, R = mesh.shape["seg"], mesh.shape["rep"]

    def body(tokens, cotangent, coefficients, w_gate, w_up, w_down):
        args = (tokens, cotangent, coefficients, w_gate, w_up, w_down)
        if w_gate.shape[1] % 128 == 0 and w_gate.shape[2] % 256 == 0 and R % 2 == 0 and S % 2 == 0 and tokens.shape[1] % 128 == 0:
            return fused(S, R, *args)
        return local(*args)

    return jax.shard_map(
        body,
        mesh=mesh,
        in_specs=placed,
        out_specs=(
            P("rep", "seg", None),
            P("rep", "seg", None),
            P("rep", "seg", None),
            P("rep", "seg", None),
        ),
        check_vma=False,
    )
```

```python
import functools

import jax
import jax.numpy as jnp
from jax import lax
from jax.experimental import pallas as pl
from jax.experimental.pallas import tpu as pltpu
from jax.sharding import PartitionSpec as P

MESH = pl.DeviceIdType.MESH
F32 = jnp.float32
BF16 = jnp.bfloat16
T = 16
GATE, UP, DOWN = 0, 1, 2


def one_hot(shape, rows_of, columns_of):
    row = lax.broadcasted_iota(jnp.int32, shape, 0)
    column = lax.broadcasted_iota(jnp.int32, shape, 1)
    return rows_of(row) == columns_of(column)


def dot(a, b):
    return jnp.dot(a, b, preferred_element_type=F32)


def dot_t(a, b):
    return lax.dot_general(a, b, (((1,), (1,)), ((), ())), preferred_element_type=F32)


def kernel(
    S, R, coef_ref, tok_hbm, cot_hbm, wg_hbm, wu_hbm, wd_hbm,
    ig_hbm, gg_hbm, gu_hbm, gd_hbm,
    x, g, xt, gt, w, msend, mfull, gsend, gall, outv, igv, cbuf, mix, fold,
    gate_s, up_s, dh_s, hid_s, dgate_s, dup_s,
    load_sem, out_sem, fsend, frecv, bsend, brecv, xsend, xrecv, ssend, srecv, csend, crecv,
):
    me = lax.axis_index("seg")
    rep = lax.axis_index("rep")
    E, rows, H = w.shape[1:]
    EL = outv.shape[1]
    chips = R // 2
    sibling = rep + 1 - 2 * lax.rem(rep, 2)

    def seg_at(k):
        return lax.rem(me + k, S)

    def seg_from(k):
        return lax.rem(me - k + S, S)

    def rep_at(k):
        return lax.rem(rep + k, R)

    def rep_from(k):
        return lax.rem(rep - k + R, R)

    def loop(lo, hi, body):
        lax.fori_loop(lo, hi, lambda i, c: (body(i), c)[1], 0)

    loads = [pltpu.make_async_copy(tok_hbm.at[0], x, load_sem.at[0]),
             pltpu.make_async_copy(cot_hbm.at[0], g, load_sem.at[1])]
    w_loads = [pltpu.make_async_copy(h, w.at[p], load_sem.at[2 + p])
               for p, h in enumerate((wg_hbm, wu_hbm, wd_hbm))]
    for c in w_loads + loads:
        c.start()

    barrier = pltpu.get_barrier_semaphore()
    for k in range(1, S):
        pl.semaphore_signal(barrier, inc=1, device_id={"seg": seg_at(k)}, device_id_type=MESH)
    for k in range(1, R):
        pl.semaphore_signal(barrier, inc=1, device_id={"rep": rep_at(k)}, device_id_type=MESH)

    coef = coef_ref[0].astype(F32)
    LANES = cbuf.shape[2]
    cbuf[rep] = dot(coef, one_hot((E, LANES), lambda i: i, lambda j: j).astype(F32))
    tall = dot(one_hot((S * T, S), lambda i: i // T, lambda j: j).astype(F32), coef)
    wide = dot(tall, one_hot((E, E * T), lambda i: i, lambda j: j // T).astype(F32))
    keep = one_hot((S * T, E * T), lambda i: i % T, lambda j: j % T)
    mix[...] = jnp.where(keep, wide, 0.0).astype(BF16)

    pl.semaphore_wait(barrier, S - 1 + R - 1)

    def coef_copy(k, owner):
        return pltpu.make_async_remote_copy(
            src_ref=cbuf.at[owner], dst_ref=cbuf.at[owner],
            send_sem=csend.at[k], recv_sem=crecv.at[k],
            device_id={"rep": rep_at(k)}, device_id_type=MESH)

    for k in range(1, R):
        coef_copy(k, rep).start()

    def merged_copy(p, k, owner):
        at = pl.ds(pl.multiple_of(owner * rows, rows), rows)
        return pltpu.make_async_remote_copy(
            src_ref=msend.at[p, seg_at(k)], dst_ref=mfull.at[p, at],
            send_sem=fsend.at[p, k], recv_sem=frecv.at[p, k],
            device_id={"seg": seg_at(k)}, device_id_type=MESH)

    for p in (GATE, UP, DOWN):
        w_loads[p].wait()

        def merge(b, p=p):
            at = pl.ds(pl.multiple_of(b * T, T), T)
            block = dot(mix[...], w[p, :, at, :].reshape(E * T, H))
            msend[p, :, at, :] = block.astype(BF16).reshape(S, T, H)

        loop(0, rows // T, merge)
        if p == GATE:
            loop(1, S, lambda k: merged_copy(GATE, k, me).start())
        mfull[p, pl.ds(pl.multiple_of(me * rows, rows), rows), :] = msend[p, me]

    for c in loads:
        c.wait()
    xt[...] = x[...].T
    gt[...] = g[...].T
    for k in range(1, R):
        coef_copy(k, rep_from(k)).wait_recv()
    every = cbuf[...].reshape(R * S, LANES)
    mine = one_hot((EL * T, LANES), lambda i: i // T + rep * EL, lambda j: j).astype(F32)
    tall = dot_t(mine, every)
    wide = dot(tall, one_hot((R * S, R * S * T), lambda i: i, lambda j: j // T).astype(F32))
    keep = one_hot((EL * T, R * S * T), lambda i: i % T, lambda j: j % T)
    fold[...] = jnp.where(keep, wide, 0.0).astype(BF16)

    def send_after(p, before):
        def step(k):
            merged_copy(before, k, me).wait_send()
            merged_copy(p, k, me).start()

        loop(1, S, step)

    Q = bsend.shape[1]
    part = rows // Q

    def piece(c):
        return pl.ds(c * part, part)

    def grad_copy(p, c, k, owner):
        return pltpu.make_async_remote_copy(
            src_ref=gsend.at[p, k, piece(c)], dst_ref=gall.at[p, rep, owner, piece(c)],
            send_sem=bsend.at[p, c, k], recv_sem=brecv.at[p, c, k],
            device_id={"seg": seg_at(k)}, device_id_type=MESH)

    def chip_copy(p, c, j, owner):
        block = gall.at[p, owner, :, piece(c)]
        return pltpu.make_async_remote_copy(
            src_ref=block, dst_ref=block,
            send_sem=xsend.at[p, c, j], recv_sem=xrecv.at[p, c, j],
            device_id={"rep": rep_at(2 * j)}, device_id_type=MESH)

    def sibling_copy(p, c, j, owner):
        block = gall.at[p, owner, :, piece(c)]
        return pltpu.make_async_remote_copy(
            src_ref=block, dst_ref=block,
            send_sem=ssend.at[p, c, j], recv_sem=srecv.at[p, c, j],
            device_id={"rep": sibling}, device_id_type=MESH)

    def make_grads(p, transposed, right):
        def one(k):
            at = pl.ds(pl.multiple_of(seg_at(k) * rows, rows), rows)
            return dot(transposed[at, :], right[...]).astype(BF16)

        def step(k):
            gsend[p, k] = one(k)

        loop(1, S, step)
        gall[p, rep, me] = one(0)

    def send(p, c):
        loop(1, S, lambda k: grad_copy(p, c, k, me).start())

    def sent(p, c):
        loop(1, S, lambda k: grad_copy(p, c, k, me).wait_send())

    send_after(UP, GATE)
    loop(1, S, lambda k: merged_copy(GATE, k, seg_from(k)).wait_recv())
    gate_s[...] = dot(x[...], mfull[GATE])
    send_after(DOWN, UP)
    loop(1, S, lambda k: merged_copy(UP, k, seg_from(k)).wait_recv())
    up_s[...] = dot(x[...], mfull[UP])
    CH = 32
    tokens = x.shape[0]

    def hidden(i):
        at = pl.ds(pl.multiple_of(i * CH, CH), CH)
        gate = gate_s[at, :]
        hid_s[at, :] = (gate * jax.nn.sigmoid(gate) * up_s[at, :]).astype(BF16)

    loop(0, tokens // CH, hidden)
    make_grads(DOWN, gt, hid_s)
    loop(1, S, lambda k: merged_copy(DOWN, k, me).wait_send())
    steps = [(p, c) for p in (DOWN, GATE, UP) for c in range(Q)]
    AHEAD = 4
    for p, c in steps[:AHEAD]:
        send(p, c)

    loop(1, S, lambda k: merged_copy(DOWN, k, seg_from(k)).wait_recv())
    dh_s[...] = dot(g[...], mfull[DOWN])

    def backward(i):
        at = pl.ds(pl.multiple_of(i * CH, CH), CH)
        gate = gate_s[at, :]
        dh = dh_s[at, :]
        sigma = jax.nn.sigmoid(gate)
        dgate_s[at, :] = (dh * up_s[at, :] * sigma * (1.0 + gate * (1.0 - sigma))).astype(BF16)
        dup_s[at, :] = (dh * (gate * sigma)).astype(BF16)

    loop(0, tokens // CH, backward)

    def input_grad(i):
        at = pl.ds(pl.multiple_of(i * rows, rows), rows)
        total = dot_t(dgate_s[...], mfull[GATE, at, :]) + dot_t(dup_s[...], mfull[UP, at, :])
        igv[:, at] = total.astype(BF16)

    ig_copy = pltpu.make_async_copy(igv, ig_hbm.at[0], out_sem.at[3])
    outs = (gg_hbm, gu_hbm, gd_hbm)
    out_copies = [ig_copy]
    make_grads(GATE, xt, dgate_s)
    for i in range(2, len(steps) + 4):
        if i - 2 + AHEAD < len(steps):
            sent(*steps[i - 2])
            send(*steps[i - 2 + AHEAD])
        if i == 3:
            make_grads(UP, xt, dup_s)
        if i == Q + 1:
            loop(0, S, input_grad)
            ig_copy.start()
        if i - 2 < len(steps):
            p, c = steps[i - 2]

            def arrived(k, p=p, c=c):
                grad_copy(p, c, k, seg_from(k)).wait_recv()

            loop(1, S, arrived)
            for j in range(1, chips):
                chip_copy(p, c, j, rep).start()
            sibling_copy(p, c, 0, rep).start()
        if 0 <= i - 3 < len(steps):
            p, c = steps[i - 3]
            for j in range(1, chips):
                chip_copy(p, c, j, rep_from(2 * j)).wait_recv()
                sibling_copy(p, c, j, rep_from(2 * j)).start()
        if 0 <= i - 4 < len(steps):
            p, c = steps[i - 4]
            for j in range(chips):
                sibling_copy(p, c, j, lax.rem(sibling - 2 * j + R, R)).wait_recv()

            def folded(b, p=p, c=c):
                at = pl.ds(pl.multiple_of(c * part + b * T, T), T)
                block = dot(fold[...], gall[p, :, :, at, :].reshape(R * S * T, H))
                outv[p, :, at, :] = block.astype(BF16).reshape(EL, T, H)

            loop(0, part // T, folded)
            if c == Q - 1:
                out = pltpu.make_async_copy(outv.at[p], outs[p], out_sem.at[p])
                out.start()
                out_copies.append(out)

    for k in range(1, R):
        coef_copy(k, rep).wait_send()
    for p, c in steps[-AHEAD:]:
        sent(p, c)
    for p, c in steps:
        for j in range(1, chips):
            chip_copy(p, c, j, rep).wait_send()
        for j in range(chips):
            sibling_copy(p, c, j, rep_from(2 * j)).wait_send()
    for out in out_copies:
        out.wait()


def place_kernel(n, *refs):
    sources, targets, held, sems = refs[:n], refs[n:2 * n], refs[2 * n:3 * n], refs[3 * n]
    loads = [pltpu.make_async_copy(a, b, sems.at[0, i]) for i, (a, b) in enumerate(zip(sources, held))]
    stores = [pltpu.make_async_copy(a, b, sems.at[1, i]) for i, (a, b) in enumerate(zip(held, targets))]
    for c in loads:
        c.start()
    for a, b in zip(loads, stores):
        a.wait()
        b.start()
    for c in stores:
        c.wait()


def place(arrays):
    n = len(arrays)
    any_spec = pl.BlockSpec(memory_space=pl.ANY)
    return pl.pallas_call(
        functools.partial(place_kernel, n),
        out_shape=tuple(jax.ShapeDtypeStruct(a.shape, a.dtype) for a in arrays),
        in_specs=[any_spec] * n,
        out_specs=(any_spec,) * n,
        scratch_shapes=[pltpu.VMEM(a.shape, a.dtype) for a in arrays] + [pltpu.SemaphoreType.DMA((2, n))],
        compiler_params=pltpu.CompilerParams(vmem_limit_bytes=58 * 1024 * 1024),
        cost_estimate=pl.CostEstimate(flops=0, bytes_accessed=4 * sum(a.size for a in arrays), transcendentals=0),
    )(*arrays)


def fused(S, R, tokens, cotangent, coefficients, w_gate, w_up, w_down):
    E, rows, H = w_gate.shape
    L, D = tokens.shape[1:]
    EL = E // R
    chips = R // 2
    lanes = -(-E // 128) * 128
    any_spec = pl.BlockSpec(memory_space=pl.ANY)
    dma = pltpu.SemaphoreType.DMA
    vmem = pltpu.VMEM
    grad = jax.ShapeDtypeStruct((EL, rows, H), BF16)
    flops = 16 * L * D * H + 2 * 3 * T * rows * H * E * S + 2 * 3 * T * rows * H * EL * R * S
    Q = 4
    made = pl.pallas_call(
        functools.partial(kernel, S, R),
        out_shape=(jax.ShapeDtypeStruct((1, L, D), BF16), grad, grad, grad),
        in_specs=[pl.BlockSpec(memory_space=vmem)] + [any_spec] * 5,
        out_specs=(any_spec,) * 4,
        scratch_shapes=[
            vmem((L, D), BF16), vmem((L, D), BF16), vmem((D, L), BF16), vmem((D, L), BF16),
            vmem((3, E, rows, H), BF16),
            vmem((3, S, rows, H), BF16),
            vmem((3, D, H), BF16),
            vmem((3, S, rows, H), BF16),
            vmem((3, R, S, rows, H), BF16),
            vmem((3, EL, rows, H), BF16),
            vmem((L, D), BF16),
            vmem((R, S, lanes), F32),
            vmem((S * T, E * T), BF16),
            vmem((EL * T, R * S * T), BF16),
            vmem((L, H), F32), vmem((L, H), F32), vmem((L, H), F32),
            vmem((L, H), BF16), vmem((L, H), BF16), vmem((L, H), BF16),
            dma((5,)), dma((4,)),
            dma((3, S)), dma((3, S)), dma((3, Q, S)), dma((3, Q, S)),
            dma((3, Q, chips)), dma((3, Q, chips)), dma((3, Q, chips)), dma((3, Q, chips)),
            dma((R,)), dma((R,)),
        ],
        compiler_params=pltpu.CompilerParams(
            collective_id=0, has_side_effects=True, vmem_limit_bytes=58 * 1024 * 1024),
        cost_estimate=pl.CostEstimate(
            flops=flops, bytes_accessed=2 * (3 * E * rows * H + 3 * L * D + 3 * EL * rows * H),
            transcendentals=2 * L * H),
    )(coefficients, tokens, cotangent, w_gate, w_up, w_down)
    return place(made)


def local(tokens, cotangent, coefficients, w_gate, w_up, w_down):
    mixing = coefficients[0]
    stacked = jnp.stack([w_gate, w_up, w_down])
    merged = jnp.einsum(
        "se,kedh->ksdh", mixing, stacked, preferred_element_type=jnp.float32
    ).astype(jnp.bfloat16)
    arrived = lax.all_to_all(merged, "seg", split_axis=1, concat_axis=2, tiled=True)
    merged_gate = arrived[0, 0]
    merged_up = arrived[1, 0]
    merged_down = arrived[2, 0]
    segment_x = tokens[0]
    segment_g = cotangent[0]
    contract = (((0,), (0,)), ((), ()))
    transposed = (((1,), (1,)), ((), ()))

    def fold_experts(pieces):
        return jnp.einsum("se,ksdh->kedh", mixing, pieces, preferred_element_type=jnp.float32)

    gate_proj = jnp.dot(segment_x, merged_gate, preferred_element_type=jnp.float32)
    up_proj = jnp.dot(segment_x, merged_up, preferred_element_type=jnp.float32)
    sigma = jax.nn.sigmoid(gate_proj)
    activated = gate_proj * sigma
    hidden = (activated * up_proj).astype(jnp.bfloat16)
    grad_down_seg = lax.dot_general(
        segment_g, hidden, contract, preferred_element_type=jnp.float32
    ).astype(jnp.bfloat16)
    down_folded = fold_experts(
        lax.all_to_all(grad_down_seg[None, None], "seg", split_axis=2, concat_axis=1, tiled=True)
    )
    down_summed = lax.psum_scatter(down_folded, "rep", scatter_dimension=1, tiled=True)
    d_hidden = jnp.dot(segment_g, merged_down, preferred_element_type=jnp.float32)
    d_gate = (d_hidden * up_proj * sigma * (1.0 + gate_proj * (1.0 - sigma))).astype(jnp.bfloat16)
    d_up = (d_hidden * activated).astype(jnp.bfloat16)
    input_grad = lax.dot_general(
        d_gate, merged_gate, transposed, preferred_element_type=jnp.float32
    )
    input_grad = input_grad + lax.dot_general(
        d_up, merged_up, transposed, preferred_element_type=jnp.float32
    )
    input_grad = input_grad.astype(jnp.bfloat16)
    grad_gate_seg = lax.dot_general(
        segment_x, d_gate, contract, preferred_element_type=jnp.float32
    ).astype(jnp.bfloat16)
    grad_up_seg = lax.dot_general(
        segment_x, d_up, contract, preferred_element_type=jnp.float32
    ).astype(jnp.bfloat16)
    pair = jnp.stack([grad_gate_seg, grad_up_seg])[:, None]
    pair_folded = fold_experts(lax.all_to_all(pair, "seg", split_axis=2, concat_axis=1, tiled=True))
    pair_summed = lax.psum_scatter(pair_folded, "rep", scatter_dimension=1, tiled=True)
    summed = jnp.concatenate([pair_summed, down_summed], axis=0)
    grads = summed.astype(jnp.bfloat16)
    return (input_grad[None], grads[0], grads[1], grads[2])


def solution(mesh):
    placed = (
        P("rep", "seg", None),
        P("rep", "seg", None),
        P("rep", None, None),
        P(None, "seg", None),
        P(None, "seg", None),
        P(None, "seg", None),
    )
    S, R = mesh.shape["seg"], mesh.shape["rep"]

    def body(tokens, cotangent, coefficients, w_gate, w_up, w_down):
        args = (tokens, cotangent, coefficients, w_gate, w_up, w_down)
        if w_gate.shape[1] % 128 == 0 and R % 2 == 0 and tokens.shape[1] % 128 == 0:
            return fused(S, R, *args)
        return local(*args)

    return jax.shard_map(
        body,
        mesh=mesh,
        in_specs=placed,
        out_specs=(
            P("rep", "seg", None),
            P("rep", "seg", None),
            P("rep", "seg", None),
            P("rep", "seg", None),
        ),
        check_vma=False,
    )
```
